256 devices in a mesh: section: 8 (over z), ep: 32 (over x, y, core).
Axes of the slice: x: 4, y: 4, z: 8, core: 2. Of those that a mesh axis runs over, the one named last changes fastest.
Arguments:
- flight_a: bfloat16 [8, 4096, 3584], P('section', 'ep'), may hold values from -6 to 6
- flight_b: bfloat16 [8, 4096, 3584], P('section', 'ep'), may hold values from -6 to 6
- routes_a: int32 [8, 1, 4096, 1], P('section', None, 'ep'), may hold values from 0 to 7; in each aligned block of 128 rows (0 to 127, 128 to 255, ..., all dimensions but the last counted through in order) at most 18 rows name the same one
- routes_b: int32 [8, 1, 4096, 1], P('section', None, 'ep'), may hold values from 0 to 7; in each aligned block of 128 rows (0 to 127, 128 to 255, ..., all dimensions but the last counted through in order) at most 18 rows name the same one
- scores_a: float32 [8, 1, 4096, 1], P('section', None, 'ep'), may hold values from 0.5 to 1.5
- scores_b: float32 [8, 1, 4096, 1], P('section', None, 'ep'), may hold values from 0.5 to 1.5
- norm_gain: float32 [8, 3584], P('section'), may hold values from 0.1 to 1.9
- w_gate: bfloat16 [8, 3584, 8192], P('section', None, 'ep'), may hold values from -0.09375 to 0.09375
- w_up: bfloat16 [8, 3584, 8192], P('section', None, 'ep'), may hold values from -0.09375 to 0.09375
- w_down: bfloat16 [8, 8192, 3584], P('section', 'ep'), may hold values from -0.1875 to 0.1875
Outputs:
- out_a: bfloat16 [8, 4096, 3584], P('section', 'ep')
- out_b: bfloat16 [8, 4096, 3584], P('section', 'ep')
The draws below stay inside these ranges and needn't reach their ends.
Inputs may be any that keep to these rules, and one draw needn't show every extreme that they name: `routes_a`: in each block of 128 rows that one device holds for one layer and step, no expert is named more than 18 times, a bound that some block reaches; a row never names one expert twice. `routes_b`: as for routes_a.
All inputs are finite; a program needn't handle non-finite values.
Results may differ from the reference program's by a relative error of at most 0.0054.
Values may be sent and summed in bfloat16 or wider, within the bound.
No kernel may reach another device: no remote copies, remote signals or barrier semaphores. Data moves between devices by JAX's collectives and lax.ppermute only.
A program may use at most 128 MiB of HBM per device.

```python
import math
import jax
import jax.numpy as jnp
import numpy as np
from jax import lax

D = 3584
FFE = 1024
ES = 4
TOPK = 1
STEPS = 1
TOK_DEV = 128
EXPERTS = 8
CAP = 18
TOKENS = 4096
LAYERS = 8
N_EP = 32


def block_levels(stream_key, dims, split, smallest, largest):
    level, own = 1.0, jax.random.fold_in(stream_key, 6)
    for dim, parts in split:
        draws = jnp.exp(jax.random.uniform(jax.random.fold_in(own, dim), (parts,), jnp.float32, smallest / len(split), largest / len(split)))
        level = level * jnp.repeat(draws, dims[dim] // parts).reshape([-1 if axis == dim else 1 for axis in range(len(dims))])
    return level


def deal_out(rng, own, number, rows, number_of, top, most, skew):
    order = jax.random.permutation(rng, number_of)
    heavy_load, common = shares(number_of, rows * top, most, skew, True), shares(number_of, rows * top, most, skew, False)
    places = jnp.arange(number_of)

    def named(tallies, rotation):
        used = int((tallies > 0).sum())
        fixed = max(1, used // 4)
        passed = fixed + (places - fixed + rotation * (used - fixed)) % max(1, number_of - fixed)
        return jnp.zeros((number_of,), jnp.int32).at[order[jnp.where(places < fixed, places, passed)]].set(jnp.asarray(tallies, jnp.int32))

    tallies = jnp.where(number % 4 == 0, named(heavy_load, number // 4), named(common, number - number // 4 - 1))
    mixed = jax.random.permutation(jax.random.fold_in(own, 3), number_of)
    source_of, taker = mixed[0:number_of // 2 * 2:2], mixed[1:number_of // 2 * 2:2]
    margin = jnp.minimum(tallies[source_of] - 1, most - tallies[taker]) // 2
    margin = jnp.where((source_of == order[0]) | (taker == order[0]) | (tallies[taker] == 0), 0, jnp.maximum(margin, 0))
    passed = jax.random.randint(jax.random.fold_in(own, 4), (number_of // 2,), 0, 1 << 20) % (margin + 1)
    tallies = tallies.at[source_of].add(-passed).at[taker].add(passed)
    members = jnp.searchsorted(jnp.cumsum(tallies), jnp.arange(rows * top), side="right").astype(jnp.int32)
    listing = members.reshape(top, rows).T
    listing = listing[jax.random.permutation(jax.random.fold_in(own, 1), rows)]
    rotation = jax.random.randint(jax.random.fold_in(own, 2), (rows, 1), 0, top)
    return jnp.take_along_axis(listing, (jnp.arange(top)[None, :] + rotation) % top, axis=1)


def shares(count, total, bound, skew, full):
    portions = [(1 << 20) // math.isqrt(rank ** skew) + 1 for rank in range(1, count + 1)]
    largest = bound if full else min(bound, max(-(-total // count), total * portions[0] // sum(portions)))
    least = 1 if total - largest >= count - 1 else 0
    given, spare = [largest] + [least] * (count - 1), total - largest - least * (count - 1)
    while spare > 0:
        movable = [i for i in range(1, count) if given[i] < largest] or [i for i in range(1, count) if given[i] < bound]
        whole, budget = sum([portions[i] for i in movable]), spare
        for i in movable:
            extra = min(bound - given[i], max(1, budget * portions[i] // whole), spare)
            given[i] = given[i] + extra
            spare = spare - extra
    return np.array(given)


def normal_values(rng, dims, scale, most, cuts=(), kind=jnp.bfloat16):
    level = block_levels(rng, dims, cuts, -0.22, 0.18) if cuts else 1.0
    drawn = jax.random.normal(rng, dims, jnp.float32) * scale * level
    return jnp.minimum(jnp.maximum(drawn, -most), most).astype(kind)


def setup_inputs(seed: int = 0) -> dict:
    keys = jax.random.split(jax.random.key(seed), 11)
    flight_a = normal_values(keys[0], (LAYERS, TOKENS, D), 1.0, 6.0, ((0, 8), (1, 32)))
    flight_b = normal_values(keys[1], (LAYERS, TOKENS, D), 1.0, 6.0, ((0, 8), (1, 32)))
    routes_a_keys = jax.random.split(jax.random.fold_in(keys[2], 1), LAYERS * STEPS * TOKENS // TOK_DEV)
    routes_a_turns = jax.random.permutation(jax.random.fold_in(keys[2], 3), LAYERS * STEPS * TOKENS // TOK_DEV)
    routes_a = jax.vmap(lambda own, number: deal_out(jax.random.fold_in(keys[2], 2), own, number, TOK_DEV, EXPERTS, TOPK, CAP, 1))(routes_a_keys, routes_a_turns).reshape((LAYERS, STEPS, TOKENS, TOPK))
    routes_b_keys = jax.random.split(jax.random.fold_in(keys[3], 1), LAYERS * STEPS * TOKENS // TOK_DEV)
    routes_b_turns = jax.random.permutation(jax.random.fold_in(keys[3], 3), LAYERS * STEPS * TOKENS // TOK_DEV)
    routes_b = jax.vmap(lambda own, number: deal_out(jax.random.fold_in(keys[3], 2), own, number, TOK_DEV, EXPERTS, TOPK, CAP, 1))(routes_b_keys, routes_b_turns).reshape((LAYERS, STEPS, TOKENS, TOPK))
    scores_a = jnp.clip(0.5 + 1.0 * jax.random.uniform(keys[4], (LAYERS, STEPS, TOKENS, TOPK), jnp.float32) ** block_levels(keys[4], (LAYERS, STEPS, TOKENS, TOPK), ((0, 8), (2, 32)), -0.2, 0.2), 0.5, 1.5)
    scores_b = jnp.clip(0.5 + 1.0 * jax.random.uniform(keys[5], (LAYERS, STEPS, TOKENS, TOPK), jnp.float32) ** block_levels(keys[5], (LAYERS, STEPS, TOKENS, TOPK), ((0, 8), (2, 32)), -0.2, 0.2), 0.5, 1.5)
    norm_gain = jnp.clip(1.0 + 0.18 * jax.random.normal(keys[6], (LAYERS, D), jnp.float32), 0.1, 1.9)
    w_gate = normal_values(keys[7], (LAYERS, D, EXPERTS * FFE), D ** -0.5, 0.09375, ((0, 8), (2, 32)))
    w_up = normal_values(keys[8], (LAYERS, D, EXPERTS * FFE), D ** -0.5, 0.09375, ((0, 8), (2, 32)))
    w_down = normal_values(keys[9], (LAYERS, EXPERTS * FFE, D), FFE ** -0.5, 0.1875, ((0, 8), (1, 32)))
    return {"flight_a": flight_a, "flight_b": flight_b, "routes_a": routes_a, "routes_b": routes_b, "scores_a": scores_a, "scores_b": scores_b, "norm_gain": norm_gain, "w_gate": w_gate, "w_up": w_up, "w_down": w_down}


EPSILON = 1e-06

def rms_norm(current, gain):
    as_float = current.astype(jnp.float32)
    inverse_rms = lax.rsqrt(lax.optimization_barrier(jnp.mean(as_float * as_float, axis=-1, keepdims=True)) + EPSILON)
    return (as_float * inverse_rms * gain).astype(jnp.bfloat16)

def moe_layer(current, expert_ids, route_weights, gain, gate_rows, up_rows, down_rows):
    normed = rms_norm(current, gain)
    row_limit = N_EP * CAP
    slice_width = FFE // ES
    feature_width = current.shape[1]

    def add_expert(total_out, expert):
        chosen = expert_ids == expert
        coefficient = lax.optimization_barrier(jnp.sum(jnp.where(chosen, route_weights, 0.0), axis=1))
        routed = jnp.any(chosen, axis=1)
        token_index = jnp.nonzero(routed, size=row_limit, fill_value=0)[0].astype(jnp.int32)
        valid_rows = jnp.arange(row_limit, dtype=jnp.int32) < jnp.sum(routed.astype(jnp.int32))
        gathered = normed[token_index]
        gate_cols = lax.dynamic_slice_in_dim(gate_rows, expert * FFE, FFE, 1)
        up_cols = lax.dynamic_slice_in_dim(up_rows, expert * FFE, FFE, 1)
        down_part = lax.dynamic_slice_in_dim(down_rows, expert * FFE, FFE, 0)
        gate_act = jnp.dot(gathered, gate_cols, preferred_element_type=jnp.float32)
        up_act = jnp.dot(gathered, up_cols, preferred_element_type=jnp.float32)
        hidden = (jax.nn.silu(gate_act) * up_act).astype(jnp.bfloat16)
        summed = jnp.zeros((row_limit, feature_width), jnp.float32)
        for piece in range(ES):
            partial_value = jnp.dot(hidden[:, piece * slice_width:(piece + 1) * slice_width], down_part[piece * slice_width:(piece + 1) * slice_width], preferred_element_type=jnp.float32)
            rounded = lax.optimization_barrier(partial_value.astype(jnp.bfloat16))
            summed = summed + rounded.astype(jnp.float32)
        scale_rows = jnp.where(valid_rows, coefficient[token_index], 0.0)
        return (total_out.at[token_index].add(summed * scale_rows[:, None]), None)
    moe_out, _ = lax.scan(add_expert, jnp.zeros(current.shape, jnp.float32), jnp.arange(EXPERTS, dtype=jnp.int32))
    return (current.astype(jnp.float32) + moe_out).astype(jnp.bfloat16)

def reference(flight_a, flight_b, routes_a, routes_b, scores_a, scores_b, norm_gain, w_gate, w_up, w_down):
    results_a = [None] * LAYERS
    results_b = [None] * LAYERS
    for start_section in range(LAYERS):
        current = flight_a[start_section]
        for step_index in range(STEPS):
            layer_index = start_section + step_index
            if layer_index < LAYERS:
                current = moe_layer(current, routes_a[layer_index, step_index], scores_a[layer_index, step_index], norm_gain[layer_index], w_gate[layer_index], w_up[layer_index], w_down[layer_index])
        results_a[(start_section + STEPS) % LAYERS] = current
        current = flight_b[start_section]
        for step_index in range(STEPS):
            layer_index = start_section - step_index
            if layer_index >= 0:
                current = moe_layer(current, routes_b[layer_index, step_index], scores_b[layer_index, step_index], norm_gain[layer_index], w_gate[layer_index], w_up[layer_index], w_down[layer_index])
        results_b[(start_section - STEPS) % LAYERS] = current
    return (jnp.stack(results_a), jnp.stack(results_b))
```

```python
import jax
import jax.numpy as jnp
from jax import lax
from jax.sharding import PartitionSpec as P

ES = 4
TOPK = 1


EPSILON = 1e-06


def from_behind(value, axis, steps):
    count = lax.axis_size(axis)
    pairs = [(source, (source + steps) % count) for source in range(count)]
    return lax.ppermute(value, axis, pairs)


def rms_norm(current, gain):
    as_float = current.astype(jnp.float32)
    inverse_rms = lax.rsqrt(jnp.mean(as_float * as_float, axis=-1, keepdims=True) + EPSILON)
    return (as_float * inverse_rms * gain).astype(jnp.bfloat16)


def routing(expert_ids, route_weights, expert_count, capacity):
    token_count, top_count = expert_ids.shape
    flat_ids = expert_ids.reshape(token_count * top_count)
    position = jnp.arange(token_count * top_count, dtype=jnp.int32)
    earlier = (flat_ids[None, :] == flat_ids[:, None]) & (position[None, :] < position[:, None])
    slot_index = jnp.sum(earlier.astype(jnp.int32), axis=1)
    column = flat_ids * capacity + slot_index
    placed = column[:, None] == jnp.arange(expert_count * capacity, dtype=jnp.int32)[None, :]
    placed = placed.reshape(token_count, top_count, expert_count * capacity)
    picker = jnp.any(placed, axis=1).astype(jnp.bfloat16)
    mixing = jnp.sum(jnp.where(placed, route_weights[:, :, None], 0.0), axis=1)
    return (picker, mixing)


def prepare(current, expert_ids, route_weights, gain, expert_count, capacity):
    normed = rms_norm(current, gain)
    picker, mixing = routing(expert_ids, route_weights, expert_count, capacity)
    feature_width = normed.shape[1]
    slotted = jnp.einsum("ts,td->sd", picker, normed, preferred_element_type=jnp.float32).astype(
        jnp.bfloat16
    )
    slotted = slotted.reshape(expert_count, 1, capacity, feature_width)
    outgoing = jnp.broadcast_to(slotted, (expert_count, ES, capacity, feature_width))
    return (outgoing.reshape(expert_count * ES, capacity, feature_width), mixing)


def expert_pass(outgoing, gate_cols, up_cols, down_part):
    received = lax.all_to_all(outgoing, "ep", split_axis=0, concat_axis=0, tiled=True)
    source_count, slot_count, feature_width = received.shape
    row_block = received.reshape(source_count * slot_count, feature_width)
    gate_act = jnp.dot(row_block, gate_cols, preferred_element_type=jnp.float32)
    up_act = jnp.dot(row_block, up_cols, preferred_element_type=jnp.float32)
    hidden = (jax.nn.silu(gate_act) * up_act).astype(jnp.bfloat16)
    partial_value = jnp.dot(hidden, down_part, preferred_element_type=jnp.float32).astype(
        jnp.bfloat16
    )
    partial_value = partial_value.reshape(source_count, slot_count, feature_width)
    return lax.all_to_all(partial_value, "ep", split_axis=0, concat_axis=0, tiled=True)


def finish(current, returned, mixing, expert_count):
    feature_width = current.shape[1]
    slot_count = returned.shape[1]
    by_slice = returned.astype(jnp.float32).reshape(expert_count, ES, slot_count, feature_width)
    summed = jnp.sum(by_slice, axis=1).reshape(expert_count * slot_count, feature_width)
    moe_out = jnp.dot(
        mixing, summed, precision=lax.Precision.HIGHEST, preferred_element_type=jnp.float32
    )
    return (current.astype(jnp.float32) + moe_out).astype(jnp.bfloat16)


def on_device(
    flight_a, flight_b, routes_a, routes_b, scores_a, scores_b, norm_gain, w_gate, w_up, w_down
):
    ep_count = lax.axis_size("ep")
    expert_count = ep_count // ES
    tok_dev = flight_a.shape[1]
    capacity = min(tok_dev, 9 * tok_dev * TOPK * ES // (8 * ep_count))
    section_index = lax.axis_index("section")
    last_section = lax.axis_size("section") - 1
    gain = norm_gain[0]
    gate_cols = w_gate[0]
    up_cols = w_up[0]
    down_part = w_down[0]
    current_a = flight_a[0]
    current_b = flight_b[0]
    outgoing_a, mixing_a = prepare(
        current_a, routes_a[0, 0], scores_a[0, 0], gain, expert_count, capacity
    )
    outgoing_b, mixing_b = prepare(
        current_b, routes_b[0, 0], scores_b[0, 0], gain, expert_count, capacity
    )
    returned_a = expert_pass(outgoing_a, gate_cols, up_cols, down_part)
    returned_b = expert_pass(outgoing_b, gate_cols, up_cols, down_part)
    updated_a = finish(current_a, returned_a, mixing_a, expert_count)
    updated_b = finish(current_b, returned_b, mixing_b, expert_count)
    current_a = jnp.where(0 <= section_index, updated_a, current_a)
    current_b = jnp.where(section_index + 0 <= last_section, updated_b, current_b)
    current_a = from_behind(current_a, "section", 1)
    current_b = from_behind(current_b, "section", -1)
    return (current_a[None], current_b[None])


def solution(mesh):
    placed = (
        P("section", "ep", None),
        P("section", "ep", None),
        P("section", None, "ep", None),
        P("section", None, "ep", None),
        P("section", None, "ep", None),
        P("section", None, "ep", None),
        P("section", None),
        P("section", None, "ep"),
        P("section", None, "ep"),
        P("section", "ep", None),
    )
    return jax.shard_map(
        on_device,
        mesh=mesh,
        in_specs=placed,
        out_specs=(P("section", "ep", None), P("section", "ep", None)),
        check_vma=False,
    )
```

```python
import jax
import jax.numpy as jnp
from jax import lax
from jax.experimental import pallas as pl
from jax.experimental.pallas import tpu as pltpu
from jax.sharding import PartitionSpec as P

ES = 4
EXPERTS = 8
EP = ES * EXPERTS
CHIPS = EP // 2
MAIN = 16
LAST = 2
EPSILON = 1e-06
F32 = jnp.float32
BF16 = jnp.bfloat16
VMEM_LIMIT = 48 * 1024 * 1024


def iota(shape, axis):
    return lax.broadcasted_iota(jnp.int32, shape, axis)


def to_column(row):
    count = row.shape[1]
    eye = iota((count, count), 0) == iota((count, count), 1)
    return jnp.sum(jnp.where(eye, row, jnp.zeros_like(row)), axis=1, keepdims=True)


def dot(left, right):
    return jnp.dot(left, right, preferred_element_type=F32)


def prepare_kernel(current_ref, ids_ref, gain_ref, send_ref):
    tokens, features = current_ref.shape
    quarter = features // ES
    ids_row = ids_ref[...]
    ids_column = to_column(ids_row)
    same = ids_column == ids_row
    earlier = same & (iota((tokens, tokens), 0) < iota((tokens, tokens), 1))
    slot_row = jnp.sum(earlier.astype(jnp.int32), axis=0, keepdims=True)
    main_row = jnp.where(slot_row < MAIN, ids_row * MAIN + slot_row, -1)
    last_row = jnp.where(slot_row < MAIN, -1, ids_row * (ES * LAST) + slot_row - MAIN)
    pick_main = (iota((EXPERTS * MAIN, tokens), 0) == main_row).astype(BF16)
    as_float = current_ref[...].astype(F32)
    inverse_rms = lax.rsqrt(jnp.mean(as_float * as_float, axis=-1, keepdims=True) + EPSILON)
    last = jnp.zeros((EXPERTS * ES * LAST, quarter), F32)
    for q in range(ES):
        columns = slice(q * quarter, (q + 1) * quarter)
        normed = (current_ref[:, columns].astype(F32) * inverse_rms * gain_ref[:, columns]).astype(
            BF16
        )
        main = dot(pick_main, normed).astype(BF16)
        for expert in range(EXPERTS):
            rows = main[expert * MAIN : (expert + 1) * MAIN]
            send_ref[2 * expert, q * MAIN : (q + 1) * MAIN, :] = rows
            send_ref[2 * expert + 1, q * MAIN : (q + 1) * MAIN, :] = rows
        place = jnp.where(last_row < 0, -1, last_row + q * LAST)
        pick_last = (iota((EXPERTS * ES * LAST, tokens), 0) == place).astype(BF16)
        last = last + dot(pick_last, normed)
    for expert in range(EXPERTS):
        rows = last[expert * ES * LAST : (expert + 1) * ES * LAST].astype(BF16)
        send_ref[2 * expert, ES * MAIN :, :] = rows
        send_ref[2 * expert + 1, ES * MAIN :, :] = rows


def prepare(current, ids_row, gain):
    tokens, features = current.shape
    quarter = features // ES
    return pl.pallas_call(
        prepare_kernel,
        out_shape=jax.ShapeDtypeStruct((CHIPS, ES * (MAIN + LAST), quarter), BF16),
        compiler_params=pltpu.CompilerParams(vmem_limit_bytes=VMEM_LIMIT),
        cost_estimate=pl.CostEstimate(
            flops=3 * tokens * tokens * features, bytes_accessed=8 * tokens * features, transcendentals=0
        ),
    )(current, ids_row, gain)


def hidden_kernel(own_ref, other_ref, gate_ref, up_ref, hidden_ref):
    quarter = own_ref.shape[2]
    count = CHIPS * (MAIN + LAST)
    for half, received in enumerate((own_ref, other_ref)):
        last = received[:, ES * MAIN :, :].astype(F32).reshape(CHIPS * ES * LAST, quarter).astype(BF16)
        gate = jnp.zeros((count, gate_ref.shape[1]), F32)
        up = jnp.zeros((count, up_ref.shape[1]), F32)
        shape = (CHIPS * LAST, CHIPS * ES * LAST)
        target = iota(shape, 0)
        source = (target // LAST) * (ES * LAST) + target % LAST
        for q in range(ES):
            main = received[:, q * MAIN : (q + 1) * MAIN, :].reshape(CHIPS * MAIN, quarter)
            pick = (iota(shape, 1) == source + q * LAST).astype(BF16)
            rows = jnp.concatenate([main, dot(pick, last).astype(BF16)], axis=0)
            gate = gate + dot(rows, gate_ref[q * quarter : (q + 1) * quarter, :])
            up = up + dot(rows, up_ref[q * quarter : (q + 1) * quarter, :])
        hidden_ref[half * count : (half + 1) * count, :] = (jax.nn.silu(gate) * up).astype(BF16)


def hidden_units(own, other, gate_cols, up_cols):
    count = 2 * CHIPS * (MAIN + LAST)
    features, width = gate_cols.shape
    return pl.pallas_call(
        hidden_kernel,
        out_shape=jax.ShapeDtypeStruct((count, width), BF16),
        compiler_params=pltpu.CompilerParams(vmem_limit_bytes=VMEM_LIMIT),
        cost_estimate=pl.CostEstimate(
            flops=4 * count * features * width,
            bytes_accessed=4 * features * width + 2 * count * features,
            transcendentals=count * width,
        ),
    )(own, other, gate_cols, up_cols)


def down_kernel(core_ref, *refs):
    hidden_refs, down_refs, back_ref = refs[:ES], refs[ES : 2 * ES], refs[2 * ES]
    count = CHIPS * (MAIN + LAST)
    tiles = down_refs[0].shape[1] // 128
    core = core_ref[0]
    for half in range(2):
        total = jnp.zeros((count, tiles * 128), F32)
        for r in range(ES):
            place = half if r < 2 else 1 - half
            total = total + dot(
                hidden_refs[r][place * count : (place + 1) * count, :], down_refs[r][...]
            )
        total = total.astype(BF16)
        target = core if half == 0 else 1 - core
        last = jnp.zeros((CHIPS * MAIN, 128), F32)
        shape = (CHIPS * MAIN, CHIPS * LAST)
        row = iota(shape, 0)
        for t in range(tiles):
            lanes = slice(t * 128, (t + 1) * 128)
            inside = row % MAIN - t * LAST
            pick = (inside >= 0) & (inside < LAST)
            pick = pick & (iota(shape, 1) == (row // MAIN) * LAST + inside)
            last = last + dot(pick.astype(BF16), total[CHIPS * MAIN :, lanes])
            for chip in range(CHIPS):
                back_ref[2 * chip + target, t * MAIN : (t + 1) * MAIN, :] = total[
                    chip * MAIN : (chip + 1) * MAIN, lanes
                ]
        last = last.astype(BF16)
        for chip in range(CHIPS):
            back_ref[2 * chip + target, tiles * MAIN :, :] = last[chip * MAIN : (chip + 1) * MAIN]


def down_product(core, hidden, down):
    rows, width = hidden[0].shape
    columns = down[0].shape[1]
    tiles = columns // 128
    return pl.pallas_call(
        down_kernel,
        out_shape=jax.ShapeDtypeStruct((EP, (tiles + 1) * MAIN, 128), BF16),
        in_specs=[pl.BlockSpec(memory_space=pltpu.SMEM)]
        + [pl.BlockSpec(memory_space=pltpu.VMEM)] * (2 * ES),
        compiler_params=pltpu.CompilerParams(vmem_limit_bytes=VMEM_LIMIT),
        cost_estimate=pl.CostEstimate(
            flops=2 * ES * rows * width * columns,
            bytes_accessed=2 * (ES * (rows + columns) * width + rows * columns),
            transcendentals=0,
        ),
    )(core, *hidden, *down)


def finish_kernel(current_ref, back_ref, ids_ref, scores_ref, out_ref):
    tokens, features = current_ref.shape
    quarter = features // ES
    tiles = quarter // 128
    ids_row = ids_ref[...]
    ids_column = to_column(ids_row)
    score = to_column(scores_ref[...])
    earlier = (ids_column == ids_row) & (iota((tokens, tokens), 1) < iota((tokens, tokens), 0))
    slot = jnp.sum(earlier.astype(jnp.int32), axis=1, keepdims=True)
    main_place = ids_column * MAIN + slot
    last_place = (EXPERTS + ids_column) * MAIN + slot - MAIN
    lane = iota((tokens, 2 * EXPERTS * MAIN), 1)
    for t in range(tiles):
        place = jnp.where(slot < MAIN, main_place, last_place + t * LAST)
        pick = (lane == place).astype(BF16)
        for q in range(ES):
            blocks = [
                back_ref[expert * ES + q, t * MAIN : (t + 1) * MAIN, :] for expert in range(EXPERTS)
            ]
            blocks += [back_ref[expert * ES + q, tiles * MAIN :, :] for expert in range(EXPERTS)]
            moe = dot(pick, jnp.concatenate(blocks, axis=0)) * score
            columns = slice(q * quarter + t * 128, q * quarter + (t + 1) * 128)
            out_ref[:, columns] = (current_ref[:, columns].astype(F32) + moe).astype(BF16)


def finish(current, back, ids_row, scores_row):
    tokens, features = current.shape
    return pl.pallas_call(
        finish_kernel,
        out_shape=jax.ShapeDtypeStruct((tokens, features), BF16),
        compiler_params=pltpu.CompilerParams(vmem_limit_bytes=VMEM_LIMIT),
        cost_estimate=pl.CostEstimate(
            flops=4 * tokens * EXPERTS * MAIN * features,
            bytes_accessed=6 * tokens * features,
            transcendentals=0,
        ),
    )(current, back, ids_row, scores_row)


def from_partner(value, offset):
    return lax.ppermute(value, "ep", [(i, i ^ offset) for i in range(EP)])


def from_behind(value, steps):
    count = lax.axis_size("section")
    return lax.ppermute(value, "section", [(i, (i + steps) % count) for i in range(count)])


def dispatch(send):
    same_core = [[2 * chip + core for chip in range(CHIPS)] for core in range(2)]
    return lax.all_to_all(
        send, "ep", split_axis=0, concat_axis=0, axis_index_groups=same_core, tiled=True
    )


def give_back(back):
    return lax.all_to_all(back, "ep", split_axis=0, concat_axis=0, tiled=True)


def on_device(
    flight_a, flight_b, routes_a, routes_b, scores_a, scores_b, norm_gain, w_gate, w_up, w_down
):
    tokens = flight_a.shape[1]
    quarter = flight_a.shape[2] // ES
    index = lax.axis_index("ep")
    core = (index % 2).astype(jnp.int32)[None]
    current_a, current_b = flight_a[0], flight_b[0]
    ids_a, ids_b = routes_a.reshape(1, tokens), routes_b.reshape(1, tokens)
    marks_a, marks_b = scores_a.reshape(1, tokens), scores_b.reshape(1, tokens)
    gate_cols, up_cols, down_rows = w_gate[0], w_up[0], w_down[0]

    down_a = []
    for offset in (0, 2, 1, 3):
        start = ((index ^ offset) % ES) * quarter
        piece = lax.dynamic_slice_in_dim(down_rows, start, quarter, 1)
        down_a.append(from_partner(piece, offset) if offset else piece)

    send_a = prepare(current_a, ids_a, norm_gain)
    own_a = dispatch(send_a)
    send_b = prepare(current_b, ids_b, norm_gain)
    own_b = dispatch(send_b)

    moved_b = from_behind(current_b, -1)
    moved_ids = from_behind(ids_b, -1)
    moved_marks = from_behind(marks_b, -1)
    down_b = [from_behind(piece, -1) for piece in down_a]

    hidden_a = hidden_units(own_a, from_partner(own_a, 1), gate_cols, up_cols)
    across_a = from_partner(hidden_a, 2)
    all_a = [hidden_a, across_a, from_partner(hidden_a, 1), from_partner(across_a, 1)]
    returned_a = give_back(down_product(core, all_a, down_a))

    hidden_b = hidden_units(own_b, from_partner(own_b, 1), gate_cols, up_cols)
    here_b = from_behind(hidden_b, -1)
    sections = lax.axis_size("section")
    pairs = [
        (s * EP + i, ((s - 1) % sections) * EP + (i ^ 2)) for s in range(sections) for i in range(EP)
    ]
    across_b = lax.ppermute(hidden_b, ("section", "ep"), pairs)
    all_b = [here_b, across_b, from_partner(here_b, 1), from_partner(across_b, 1)]
    returned_b = give_back(down_product(core, all_b, down_b))

    updated_a = from_behind(finish(current_a, returned_a, ids_a, marks_a), 1)
    updated_b = finish(moved_b, returned_b, moved_ids, moved_marks)
    return (updated_a[None], updated_b[None])


def solution(mesh):
    placed = (
        P("section", "ep", None),
        P("section", "ep", None),
        P("section", None, "ep", None),
        P("section", None, "ep", None),
        P("section", None, "ep", None),
        P("section", None, "ep", None),
        P("section", None),
        P("section", None, "ep"),
        P("section", None, "ep"),
        P("section", "ep", None),
    )
    return jax.shard_map(
        on_device,
        mesh=mesh,
        in_specs=placed,
        out_specs=(P("section", "ep", None), P("section", "ep", None)),
        check_vma=False,
    )
```

```python
import jax
import jax.numpy as jnp
from jax import lax
from jax.experimental import pallas as pl
from jax.experimental.pallas import tpu as pltpu
from jax.sharding import PartitionSpec as P

ES = 4
EXPERTS = 8
EP = ES * EXPERTS
CHIPS = EP // 2
MAIN = 16
LAST = 2
EPSILON = 1e-06
F32 = jnp.float32
BF16 = jnp.bfloat16
VMEM_LIMIT = 48 * 1024 * 1024


def iota(shape, axis):
    return lax.broadcasted_iota(jnp.int32, shape, axis)


def to_column(row):
    count = row.shape[1]
    eye = iota((count, count), 0) == iota((count, count), 1)
    return jnp.sum(jnp.where(eye, row, jnp.zeros_like(row)), axis=1, keepdims=True)


def dot(left, right):
    return jnp.dot(left, right, preferred_element_type=F32)


def prepare_kernel(current_ref, ids_ref, gain_ref, send_ref):
    tokens, features = current_ref.shape
    quarter = features // ES
    ids_row = ids_ref[...]
    ids_column = to_column(ids_row)
    same = ids_column == ids_row
    earlier = same & (iota((tokens, tokens), 0) < iota((tokens, tokens), 1))
    slot_row = jnp.sum(earlier.astype(jnp.int32), axis=0, keepdims=True)
    main_row = jnp.where(slot_row < MAIN, ids_row * MAIN + slot_row, -1)
    last_row = jnp.where(slot_row < MAIN, -1, ids_row * (ES * LAST) + slot_row - MAIN)
    pick_main = (iota((EXPERTS * MAIN, tokens), 0) == main_row).astype(BF16)
    as_float = current_ref[...].astype(F32)
    inverse_rms = lax.rsqrt(jnp.mean(as_float * as_float, axis=-1, keepdims=True) + EPSILON)
    last = jnp.zeros((EXPERTS * ES * LAST, quarter), F32)
    for q in range(ES):
        columns = slice(q * quarter, (q + 1) * quarter)
        normed = (current_ref[:, columns].astype(F32) * inverse_rms * gain_ref[:, columns]).astype(
            BF16
        )
        main = dot(pick_main, normed).astype(BF16)
        for expert in range(EXPERTS):
            rows = main[expert * MAIN : (expert + 1) * MAIN]
            send_ref[2 * expert, q * MAIN : (q + 1) * MAIN, :] = rows
            send_ref[2 * expert + 1, q * MAIN : (q + 1) * MAIN, :] = rows
        place = jnp.where(last_row < 0, -1, last_row + q * LAST)
        pick_last = (iota((EXPERTS * ES * LAST, tokens), 0) == place).astype(BF16)
        last = last + dot(pick_last, normed)
    for expert in range(EXPERTS):
        rows = last[expert * ES * LAST : (expert + 1) * ES * LAST].astype(BF16)
        send_ref[2 * expert, ES * MAIN :, :] = rows
        send_ref[2 * expert + 1, ES * MAIN :, :] = rows


def prepare(current, ids_row, gain):
    tokens, features = current.shape
    quarter = features // ES
    return pl.pallas_call(
        prepare_kernel,
        out_shape=jax.ShapeDtypeStruct((CHIPS, ES * (MAIN + LAST), quarter), BF16),
        compiler_params=pltpu.CompilerParams(vmem_limit_bytes=VMEM_LIMIT),
        cost_estimate=pl.CostEstimate(
            flops=3 * tokens * tokens * features, bytes_accessed=8 * tokens * features, transcendentals=0
        ),
    )(current, ids_row, gain)


def hidden_kernel(own_ref, other_ref, gate_ref, up_ref, hidden_ref):
    quarter = own_ref.shape[2]
    count = CHIPS * (MAIN + LAST)
    for half, received in enumerate((own_ref, other_ref)):
        last = received[:, ES * MAIN :, :].astype(F32).reshape(CHIPS * ES * LAST, quarter).astype(BF16)
        gate = jnp.zeros((count, gate_ref.shape[1]), F32)
        up = jnp.zeros((count, up_ref.shape[1]), F32)
        shape = (CHIPS * LAST, CHIPS * ES * LAST)
        target = iota(shape, 0)
        source = (target // LAST) * (ES * LAST) + target % LAST
        for q in range(ES):
            main = received[:, q * MAIN : (q + 1) * MAIN, :].reshape(CHIPS * MAIN, quarter)
            pick = (iota(shape, 1) == source + q * LAST).astype(BF16)
            rows = jnp.concatenate([main, dot(pick, last).astype(BF16)], axis=0)
            gate = gate + dot(rows, gate_ref[q * quarter : (q + 1) * quarter, :])
            up = up + dot(rows, up_ref[q * quarter : (q + 1) * quarter, :])
        hidden_ref[half * count : (half + 1) * count, :] = (jax.nn.silu(gate) * up).astype(BF16)


def hidden_units(own, other, gate_cols, up_cols):
    count = 2 * CHIPS * (MAIN + LAST)
    features, width = gate_cols.shape
    return pl.pallas_call(
        hidden_kernel,
        out_shape=jax.ShapeDtypeStruct((count, width), BF16),
        compiler_params=pltpu.CompilerParams(vmem_limit_bytes=VMEM_LIMIT),
        cost_estimate=pl.CostEstimate(
            flops=4 * count * features * width,
            bytes_accessed=4 * features * width + 2 * count * features,
            transcendentals=count * width,
        ),
    )(own, other, gate_cols, up_cols)


def down_kernel(core_ref, *refs):
    hidden_refs, down_refs, back_ref = refs[:ES], refs[ES : 2 * ES], refs[2 * ES]
    count = CHIPS * (MAIN + LAST)
    tiles = down_refs[0].shape[1] // 128
    core = core_ref[0]
    for half in range(2):
        total = jnp.zeros((count, tiles * 128), F32)
        for r in range(ES):
            place = half if r < 2 else 1 - half
            total = total + dot(
                hidden_refs[r][place * count : (place + 1) * count, :], down_refs[r][...]
            )
        total = total.astype(BF16)
        target = core if half == 0 else 1 - core
        last = jnp.zeros((CHIPS * MAIN, 128), F32)
        shape = (CHIPS * MAIN, CHIPS * LAST)
        row = iota(shape, 0)
        for t in range(tiles):
            lanes = slice(t * 128, (t + 1) * 128)
            inside = row % MAIN - t * LAST
            pick = (inside >= 0) & (inside < LAST)
            pick = pick & (iota(shape, 1) == (row // MAIN) * LAST + inside)
            last = last + dot(pick.astype(BF16), total[CHIPS * MAIN :, lanes])
            for chip in range(CHIPS):
                back_ref[2 * chip + target, t * MAIN : (t + 1) * MAIN, :] = total[
                    chip * MAIN : (chip + 1) * MAIN, lanes
                ]
        last = last.astype(BF16)
        for chip in range(CHIPS):
            back_ref[2 * chip + target, tiles * MAIN :, :] = last[chip * MAIN : (chip + 1) * MAIN]


def down_product(core, hidden, down):
    rows, width = hidden[0].shape
    columns = down[0].shape[1]
    tiles = columns // 128
    return pl.pallas_call(
        down_kernel,
        out_shape=jax.ShapeDtypeStruct((EP, (tiles + 1) * MAIN, 128), BF16),
        in_specs=[pl.BlockSpec(memory_space=pltpu.SMEM)]
        + [pl.BlockSpec(memory_space=pltpu.VMEM)] * (2 * ES),
        compiler_params=pltpu.CompilerParams(vmem_limit_bytes=VMEM_LIMIT),
        cost_estimate=pl.CostEstimate(
            flops=2 * ES * rows * width * columns,
            bytes_accessed=2 * (ES * (rows + columns) * width + rows * columns),
            transcendentals=0,
        ),
    )(core, *hidden, *down)


def finish_kernel(current_ref, back_ref, ids_ref, scores_ref, out_ref):
    tokens, features = current_ref.shape
    quarter = features // ES
    tiles = quarter // 128
    ids_row = ids_ref[...]
    ids_column = to_column(ids_row)
    score = to_column(scores_ref[...])
    earlier = (ids_column == ids_row) & (iota((tokens, tokens), 1) < iota((tokens, tokens), 0))
    slot = jnp.sum(earlier.astype(jnp.int32), axis=1, keepdims=True)
    main_place = ids_column * MAIN + slot
    last_place = (EXPERTS + ids_column) * MAIN + slot - MAIN
    lane = iota((tokens, 2 * EXPERTS * MAIN), 1)
    for t in range(tiles):
        place = jnp.where(slot < MAIN, main_place, last_place + t * LAST)
        pick = (lane == place).astype(BF16)
        for q in range(ES):
            blocks = [
                back_ref[expert * ES + q, t * MAIN : (t + 1) * MAIN, :] for expert in range(EXPERTS)
            ]
            blocks += [back_ref[expert * ES + q, tiles * MAIN :, :] for expert in range(EXPERTS)]
            moe = dot(pick, jnp.concatenate(blocks, axis=0)) * score
            columns = slice(q * quarter + t * 128, q * quarter + (t + 1) * 128)
            out_ref[:, columns] = (current_ref[:, columns].astype(F32) + moe).astype(BF16)


def finish(current, back, ids_row, scores_row):
    tokens, features = current.shape
    return pl.pallas_call(
        finish_kernel,
        out_shape=jax.ShapeDtypeStruct((tokens, features), BF16),
        compiler_params=pltpu.CompilerParams(vmem_limit_bytes=VMEM_LIMIT),
        cost_estimate=pl.CostEstimate(
            flops=4 * tokens * EXPERTS * MAIN * features,
            bytes_accessed=6 * tokens * features,
            transcendentals=0,
        ),
    )(current, back, ids_row, scores_row)


def from_partner(value, offset):
    return lax.ppermute(value, "ep", [(i, i ^ offset) for i in range(EP)])


def from_behind(value, steps):
    count = lax.axis_size("section")
    return lax.ppermute(value, "section", [(i, (i + steps) % count) for i in range(count)])


def dispatch(send):
    same_core = [[2 * chip + core for chip in range(CHIPS)] for core in range(2)]
    return lax.all_to_all(
        send, "ep", split_axis=0, concat_axis=0, axis_index_groups=same_core, tiled=True
    )


def give_back(back):
    return lax.all_to_all(back, "ep", split_axis=0, concat_axis=0, tiled=True)


def on_device(
    flight_a, flight_b, routes_a, routes_b, scores_a, scores_b, norm_gain, w_gate, w_up, w_down
):
    tokens = flight_a.shape[1]
    quarter = flight_a.shape[2] // ES
    index = lax.axis_index("ep")
    core = (index % 2).astype(jnp.int32)[None]
    current_a, current_b = flight_a[0], flight_b[0]
    ids_a, ids_b = routes_a.reshape(1, tokens), routes_b.reshape(1, tokens)
    marks_a, marks_b = scores_a.reshape(1, tokens), scores_b.reshape(1, tokens)
    gate_cols, up_cols, down_rows = w_gate[0], w_up[0], w_down[0]

    down_a = []
    for offset in (0, 2, 1, 3):
        start = ((index ^ offset) % ES) * quarter
        piece = lax.dynamic_slice_in_dim(down_rows, start, quarter, 1)
        down_a.append(from_partner(piece, offset) if offset else piece)

    own_a = dispatch(prepare(current_a, ids_a, norm_gain))
    send_b = prepare(current_b, ids_b, norm_gain)

    moved = [from_behind(value, -1) for value in (current_b, ids_b, marks_b, down_a[0])]
    own_a, send_b, down_a, moved = lax.optimization_barrier((own_a, send_b, down_a, moved))
    own_b = dispatch(send_b)
    down_b = [moved[3]] + [from_behind(piece, -1) for piece in down_a[1:]]

    hidden_a = hidden_units(own_a, from_partner(own_a, 1), gate_cols, up_cols)
    across_a = from_partner(hidden_a, 2)
    all_a = [hidden_a, across_a, from_partner(hidden_a, 1), from_partner(across_a, 1)]
    back_a = down_product(core, all_a, down_a)

    own_b, back_a, down_b = lax.optimization_barrier((own_b, back_a, down_b))
    returned_a = give_back(back_a)
    hidden_b = hidden_units(own_b, from_partner(own_b, 1), gate_cols, up_cols)
    here_b = from_behind(hidden_b, -1)
    sections = lax.axis_size("section")
    pairs = [
        (s * EP + i, ((s - 1) % sections) * EP + (i ^ 2)) for s in range(sections) for i in range(EP)
    ]
    across_b = lax.ppermute(hidden_b, ("section", "ep"), pairs)
    all_b = [here_b, across_b, from_partner(here_b, 1), from_partner(across_b, 1)]
    back_b = down_product(core, all_b, down_b)

    updated_a = finish(current_a, returned_a, ids_a, marks_a)
    updated_a, back_b = lax.optimization_barrier((updated_a, back_b))
    returned_b = give_back(back_b)
    updated_a = from_behind(updated_a, 1)
    moved_b, moved_ids, moved_marks = moved[:3]
    updated_b = finish(moved_b, returned_b, moved_ids, moved_marks)
    return (updated_a[None], updated_b[None])


def solution(mesh):
    placed = (
        P("section", "ep", None),
        P("section", "ep", None),
        P("section", None, "ep", None),
        P("section", None, "ep", None),
        P("section", None, "ep", None),
        P("section", None, "ep", None),
        P("section", None),
        P("section", None, "ep"),
        P("section", None, "ep"),
        P("section", "ep", None),
    )
    return jax.shard_map(
        on_device,
        mesh=mesh,
        in_specs=placed,
        out_specs=(P("section", "ep", None), P("section", "ep", None)),
        check_vma=False,
    )
```

```python
import jax
import jax.numpy as jnp
from jax import lax
from jax.experimental import pallas as pl
from jax.experimental.pallas import tpu as pltpu
from jax.sharding import PartitionSpec as P

ES = 4
EXPERTS = 8
EP = ES * EXPERTS
CHIPS = EP // 2
MAIN = 16
LAST = 2
SPARE = 2
EPSILON = 1e-06
F32 = jnp.float32
BF16 = jnp.bfloat16
VMEM_LIMIT = 48 * 1024 * 1024


def iota(shape, axis):
    return lax.broadcasted_iota(jnp.int32, shape, axis)


def to_column(row):
    count = row.shape[1]
    eye = iota((count, count), 0) == iota((count, count), 1)
    return jnp.sum(jnp.where(eye, row, jnp.zeros_like(row)), axis=1, keepdims=True)


def dot(left, right):
    return jnp.dot(left, right, preferred_element_type=F32)


def prepare_kernel(current_ref, ids_ref, gain_ref, send_ref):
    tokens, features = current_ref.shape
    quarter = features // ES
    ids_row = ids_ref[...]
    ids_column = to_column(ids_row)
    same = ids_column == ids_row
    earlier = same & (iota((tokens, tokens), 0) < iota((tokens, tokens), 1))
    slot_row = jnp.sum(earlier.astype(jnp.int32), axis=0, keepdims=True)
    main_row = jnp.where(slot_row < MAIN, ids_row * MAIN + slot_row, -1)
    last_row = jnp.where(slot_row < MAIN, -1, ids_row * (ES * LAST) + slot_row - MAIN)
    pick_main = (iota((EXPERTS * MAIN, tokens), 0) == main_row).astype(BF16)
    as_float = current_ref[...].astype(F32)
    inverse_rms = lax.rsqrt(jnp.mean(as_float * as_float, axis=-1, keepdims=True) + EPSILON)
    last = jnp.zeros((EXPERTS * ES * LAST, quarter), F32)
    for q in range(ES):
        columns = slice(q * quarter, (q + 1) * quarter)
        normed = (current_ref[:, columns].astype(F32) * inverse_rms * gain_ref[:, columns]).astype(
            BF16
        )
        main = dot(pick_main, normed).astype(BF16)
        for expert in range(EXPERTS):
            rows = main[expert * MAIN : (expert + 1) * MAIN]
            send_ref[2 * expert, q * MAIN : (q + 1) * MAIN, :] = rows
            send_ref[2 * expert + 1, q * MAIN : (q + 1) * MAIN, :] = rows
        place = jnp.where(last_row < 0, -1, last_row + q * LAST)
        pick_last = (iota((EXPERTS * ES * LAST, tokens), 0) == place).astype(BF16)
        last = last + dot(pick_last, normed)
    for expert in range(EXPERTS):
        rows = last[expert * ES * LAST : (expert + 1) * ES * LAST].astype(BF16)
        send_ref[2 * expert, ES * MAIN :, :] = rows
        send_ref[2 * expert + 1, ES * MAIN :, :] = rows


def prepare(current, ids_row, gain):
    tokens, features = current.shape
    quarter = features // ES
    return pl.pallas_call(
        prepare_kernel,
        out_shape=jax.ShapeDtypeStruct((CHIPS, ES * (MAIN + LAST), quarter), BF16),
        compiler_params=pltpu.CompilerParams(vmem_limit_bytes=VMEM_LIMIT),
        cost_estimate=pl.CostEstimate(
            flops=3 * tokens * tokens * features, bytes_accessed=8 * tokens * features, transcendentals=0
        ),
    )(current, ids_row, gain)


def hidden_kernel(own_ref, other_ref, gate_ref, up_ref, hidden_ref):
    quarter = own_ref.shape[2]
    count = CHIPS * (MAIN + LAST)
    for half, received in enumerate((own_ref, other_ref)):
        last = received[:, ES * MAIN :, :].astype(F32).reshape(CHIPS * ES * LAST, quarter).astype(BF16)
        gate = jnp.zeros((count, gate_ref.shape[1]), F32)
        up = jnp.zeros((count, up_ref.shape[1]), F32)
        shape = (CHIPS * LAST, CHIPS * ES * LAST)
        target = iota(shape, 0)
        source = (target // LAST) * (ES * LAST) + target % LAST
        for q in range(ES):
            main = received[:, q * MAIN : (q + 1) * MAIN, :].reshape(CHIPS * MAIN, quarter)
            pick = (iota(shape, 1) == source + q * LAST).astype(BF16)
            rows = jnp.concatenate([main, dot(pick, last).astype(BF16)], axis=0)
            gate = gate + dot(rows, gate_ref[q * quarter : (q + 1) * quarter, :])
            up = up + dot(rows, up_ref[q * quarter : (q + 1) * quarter, :])
        hidden_ref[half * count : (half + 1) * count, :] = (jax.nn.silu(gate) * up).astype(BF16)


def hidden_units(own, other, gate_cols, up_cols):
    count = 2 * CHIPS * (MAIN + LAST)
    features, width = gate_cols.shape
    return pl.pallas_call(
        hidden_kernel,
        out_shape=jax.ShapeDtypeStruct((count, width), BF16),
        compiler_params=pltpu.CompilerParams(vmem_limit_bytes=VMEM_LIMIT),
        cost_estimate=pl.CostEstimate(
            flops=4 * count * features * width,
            bytes_accessed=4 * features * width + 2 * count * features,
            transcendentals=count * width,
        ),
    )(own, other, gate_cols, up_cols)


def down_kernel(core_ref, mine_ref, theirs_ref, down_ref, other_down_ref, back_ref):
    count = CHIPS * (MAIN + LAST)
    wide = back_ref.shape[1] // MAIN * 128 - SPARE * 128
    tiles = wide // 128
    core = core_ref[0]
    columns = pl.ds(pl.multiple_of(core * wide, 128), wide)
    shape = (CHIPS * SPARE * MAIN, CHIPS * LAST)
    row = iota(shape, 0)
    for half in range(2):
        here, there = half * count, (1 - half) * count
        total = dot(mine_ref[here : here + count, :], down_ref[:, columns])
        total = total + dot(theirs_ref[there : there + count, :], other_down_ref[:, columns])
        total = total.astype(BF16)
        target = core if half == 0 else 1 - core
        last = jnp.zeros((CHIPS * SPARE * MAIN, 128), F32)
        for t in range(tiles):
            lanes = slice(t * 128, (t + 1) * 128)
            inside = row % (SPARE * MAIN) - t * LAST
            pick = (inside >= 0) & (inside < LAST)
            pick = pick & (iota(shape, 1) == (row // (SPARE * MAIN)) * LAST + inside)
            last = last + dot(pick.astype(BF16), total[CHIPS * MAIN :, lanes])
            for chip in range(CHIPS):
                back_ref[2 * chip + target, t * MAIN : (t + 1) * MAIN, :] = total[
                    chip * MAIN : (chip + 1) * MAIN, lanes
                ]
        last = last.astype(BF16)
        for chip in range(CHIPS):
            back_ref[2 * chip + target, tiles * MAIN :, :] = last[
                chip * SPARE * MAIN : (chip + 1) * SPARE * MAIN
            ]


def down_product(core, mine, theirs, down, other_down):
    rows, width = mine.shape
    columns = down.shape[1] // 2
    tiles = columns // 128
    return pl.pallas_call(
        down_kernel,
        out_shape=jax.ShapeDtypeStruct((EP, (tiles + SPARE) * MAIN, 128), BF16),
        in_specs=[pl.BlockSpec(memory_space=pltpu.SMEM)]
        + [pl.BlockSpec(memory_space=pltpu.VMEM)] * 4,
        compiler_params=pltpu.CompilerParams(vmem_limit_bytes=VMEM_LIMIT),
        cost_estimate=pl.CostEstimate(
            flops=4 * rows * width * columns,
            bytes_accessed=2 * (2 * (rows + 2 * columns) * width + rows * columns),
            transcendentals=0,
        ),
    )(core, mine, theirs, down, other_down)


def finish_kernel(current_ref, back_ref, ids_ref, scores_ref, out_ref):
    tokens, features = current_ref.shape
    tiles = features // 256
    ids_row = ids_ref[...]
    ids_column = to_column(ids_row)
    score = to_column(scores_ref[...])
    earlier = (ids_column == ids_row) & (iota((tokens, tokens), 1) < iota((tokens, tokens), 0))
    slot = jnp.sum(earlier.astype(jnp.int32), axis=1, keepdims=True)
    lane = iota((tokens, 2 * EXPERTS * MAIN), 1)
    pick_main = (lane // (2 * MAIN) == ids_column) & (lane % MAIN == slot)
    pick_main = pick_main.astype(BF16)
    lane = iota((tokens, 2 * EXPERTS * SPARE * MAIN), 1)
    in_expert = lane // (2 * SPARE * MAIN) == ids_column
    in_expert = in_expert & (slot >= MAIN)
    in_block = lane % (SPARE * MAIN)

    def rows(first, count):
        sides = [
            jnp.concatenate(
                [back_ref[2 * source + core, first : first + count, :] for source in range(CHIPS)],
                axis=0,
            )
            for core in range(2)
        ]
        return jnp.concatenate(sides, axis=1)

    last = rows(tiles * MAIN, SPARE * MAIN)
    for t in range(tiles):
        pick_last = in_expert & (in_block == t * LAST + slot - MAIN)
        moe = dot(pick_main, rows(t * MAIN, MAIN)) + dot(pick_last.astype(BF16), last)
        moe = moe * score
        for core in range(2):
            start = core * (features // 2) + t * 128
            columns = slice(start, start + 128)
            out_ref[:, columns] = (
                current_ref[:, columns].astype(F32) + moe[:, core * 128 : (core + 1) * 128]
            ).astype(BF16)


def finish(current, back, ids_row, scores_row):
    tokens, features = current.shape
    return pl.pallas_call(
        finish_kernel,
        out_shape=jax.ShapeDtypeStruct((tokens, features), BF16),
        compiler_params=pltpu.CompilerParams(vmem_limit_bytes=VMEM_LIMIT),
        cost_estimate=pl.CostEstimate(
            flops=4 * tokens * EXPERTS * MAIN * features,
            bytes_accessed=8 * tokens * features,
            transcendentals=0,
        ),
    )(current, back, ids_row, scores_row)


def swap_cores(value):
    return lax.ppermute(value, "ep", [(i, i ^ 1) for i in range(EP)])


def from_behind(value, steps):
    count = lax.axis_size("section")
    return lax.ppermute(value, "section", [(i, (i + steps) % count) for i in range(count)])


def dispatch(send):
    same_core = [[2 * chip + core for chip in range(CHIPS)] for core in range(2)]
    return lax.all_to_all(
        send, "ep", split_axis=0, concat_axis=0, axis_index_groups=same_core, tiled=True
    )


def give_back(back):
    return lax.all_to_all(back, "ep", split_axis=0, concat_axis=0, tiled=True)


def on_device(
    flight_a, flight_b, routes_a, routes_b, scores_a, scores_b, norm_gain, w_gate, w_up, w_down
):
    tokens = flight_a.shape[1]
    core = (lax.axis_index("ep") % 2).astype(jnp.int32)[None]
    current_a, current_b = flight_a[0], flight_b[0]
    ids_a, ids_b = routes_a.reshape(1, tokens), routes_b.reshape(1, tokens)
    marks_a, marks_b = scores_a.reshape(1, tokens), scores_b.reshape(1, tokens)
    gate_cols, up_cols, down = w_gate[0], w_up[0], w_down[0]

    own_a = dispatch(prepare(current_a, ids_a, norm_gain))
    send_b = prepare(current_b, ids_b, norm_gain)
    middle = down.shape[0] // 2
    upper = from_behind(down[:middle], -1)
    own_a, send_b, upper = lax.optimization_barrier((own_a, send_b, upper))
    own_b = dispatch(send_b)

    lower = from_behind(down[middle:], -1)
    hidden_a = hidden_units(own_a, swap_cores(own_a), gate_cols, up_cols)
    hidden_a, lower = lax.optimization_barrier((hidden_a, lower))
    back_a = down_product(core, hidden_a, swap_cores(hidden_a), down, swap_cores(down))
    moved_down = jnp.concatenate([upper, lower], axis=0)
    own_b, back_a, moved_down = lax.optimization_barrier((own_b, back_a, moved_down))

    returned_a = give_back(back_a)
    hidden_b = hidden_units(own_b, swap_cores(own_b), gate_cols, up_cols)
    hidden_b = from_behind(hidden_b, -1)
    back_b = down_product(core, hidden_b, swap_cores(hidden_b), moved_down, swap_cores(moved_down))
    moved_b, moved_ids, moved_marks = [
        from_behind(value, -1) for value in (current_b, ids_b, marks_b)
    ]

    marks_a, back_b = lax.optimization_barrier((marks_a, back_b))
    returned_b = give_back(back_b)
    updated_a = finish(current_a, returned_a, ids_a, marks_a)
    updated_a = from_behind(updated_a, 1)
    updated_b = finish(moved_b, returned_b, moved_ids, moved_marks)
    return (updated_a[None], updated_b[None])


def solution(mesh):
    placed = (
        P("section", "ep", None),
        P("section", "ep", None),
        P("section", None, "ep", None),
        P("section", None, "ep", None),
        P("section", None, "ep", None),
        P("section", None, "ep", None),
        P("section", None),
        P("section", None, "ep"),
        P("section", None, "ep"),
        P("section", "ep", None),
    )
    return jax.shard_map(
        on_device,
        mesh=mesh,
        in_specs=placed,
        out_specs=(P("section", "ep", None), P("section", "ep", None)),
        check_vma=False,
    )
```

```python
import functools

import jax
import jax.numpy as jnp
from jax import lax
from jax.experimental import pallas as pl
from jax.experimental.pallas import tpu as pltpu
from jax.sharding import PartitionSpec as P

ES = 4
EXPERTS = 8
EP = ES * EXPERTS
CHIPS = EP // 2
MAIN = 16
LAST = 2
ORDER = (2, 10, 0, 14, 6, 5, 3, 8, 7, 11, 15, 1, 12, 13, 9, 4)
EPSILON = 1e-06
F32 = jnp.float32
BF16 = jnp.bfloat16
VMEM_LIMIT = 48 * 1024 * 1024


def iota(shape, axis):
    return lax.broadcasted_iota(jnp.int32, shape, axis)


def to_column(row):
    count = row.shape[1]
    eye = iota((count, count), 0) == iota((count, count), 1)
    return jnp.sum(jnp.where(eye, row, jnp.zeros_like(row)), axis=1, keepdims=True)


def dot(left, right):
    return jnp.dot(left, right, preferred_element_type=F32)


def prepare_kernel(current_ref, ids_ref, gain_ref, send_ref):
    tokens, features = current_ref.shape
    quarter = features // ES
    ids_row = ids_ref[...]
    ids_column = to_column(ids_row)
    same = ids_column == ids_row
    earlier = same & (iota((tokens, tokens), 0) < iota((tokens, tokens), 1))
    slot_row = jnp.sum(earlier.astype(jnp.int32), axis=0, keepdims=True)
    main_row = jnp.where(slot_row < MAIN, ids_row * MAIN + slot_row, -1)
    last_row = jnp.where(slot_row < MAIN, -1, ids_row * (ES * LAST) + slot_row - MAIN)
    pick_main = (iota((EXPERTS * MAIN, tokens), 0) == main_row).astype(BF16)
    as_float = current_ref[...].astype(F32)
    inverse_rms = lax.rsqrt(jnp.mean(as_float * as_float, axis=-1, keepdims=True) + EPSILON)
    last = jnp.zeros((EXPERTS * ES * LAST, quarter), F32)
    for q in range(ES):
        columns = slice(q * quarter, (q + 1) * quarter)
        normed = (current_ref[:, columns].astype(F32) * inverse_rms * gain_ref[:, columns]).astype(
            BF16
        )
        main = dot(pick_main, normed).astype(BF16)
        for expert in range(EXPERTS):
            rows = main[expert * MAIN : (expert + 1) * MAIN]
            for chip in (2 * expert, 2 * expert + 1):
                send_ref[ORDER.index(chip), q * MAIN : (q + 1) * MAIN, :] = rows
        place = jnp.where(last_row < 0, -1, last_row + q * LAST)
        pick_last = (iota((EXPERTS * ES * LAST, tokens), 0) == place).astype(BF16)
        last = last + dot(pick_last, normed)
    for expert in range(EXPERTS):
        rows = last[expert * ES * LAST : (expert + 1) * ES * LAST].astype(BF16)
        for chip in (2 * expert, 2 * expert + 1):
            send_ref[ORDER.index(chip), ES * MAIN :, :] = rows


def prepare(current, ids_row, gain):
    tokens, features = current.shape
    quarter = features // ES
    return pl.pallas_call(
        prepare_kernel,
        out_shape=jax.ShapeDtypeStruct((CHIPS, ES * (MAIN + LAST), quarter), BF16),
        compiler_params=pltpu.CompilerParams(vmem_limit_bytes=VMEM_LIMIT),
        cost_estimate=pl.CostEstimate(
            flops=3 * tokens * tokens * features, bytes_accessed=8 * tokens * features, transcendentals=0
        ),
    )(current, ids_row, gain)


def hidden_kernel(own_ref, other_ref, gate_ref, up_ref, mine_ref, give_ref):
    quarter = own_ref.shape[2]
    count = CHIPS * (MAIN + LAST)
    for received, hidden_ref in ((own_ref, mine_ref), (other_ref, give_ref)):
        last = received[:, ES * MAIN :, :].astype(F32).reshape(CHIPS * ES * LAST, quarter).astype(BF16)
        gate = jnp.zeros((count, gate_ref.shape[1]), F32)
        up = jnp.zeros((count, up_ref.shape[1]), F32)
        shape = (CHIPS * LAST, CHIPS * ES * LAST)
        target = iota(shape, 0)
        source = (target // LAST) * (ES * LAST) + target % LAST
        for q in range(ES):
            main = received[:, q * MAIN : (q + 1) * MAIN, :].reshape(CHIPS * MAIN, quarter)
            pick = (iota(shape, 1) == source + q * LAST).astype(BF16)
            rows = jnp.concatenate([main, dot(pick, last).astype(BF16)], axis=0)
            gate = gate + dot(rows, gate_ref[q * quarter : (q + 1) * quarter, :])
            up = up + dot(rows, up_ref[q * quarter : (q + 1) * quarter, :])
        hidden_ref[...] = (jax.nn.silu(gate) * up).astype(BF16)


def hidden_units(own, other, gate_cols, up_cols):
    count = CHIPS * (MAIN + LAST)
    features, width = gate_cols.shape
    return pl.pallas_call(
        hidden_kernel,
        out_shape=[jax.ShapeDtypeStruct((count, width), BF16)] * 2,
        compiler_params=pltpu.CompilerParams(vmem_limit_bytes=VMEM_LIMIT),
        cost_estimate=pl.CostEstimate(
            flops=8 * count * features * width,
            bytes_accessed=4 * features * width + 4 * count * features,
            transcendentals=2 * count * width,
        ),
    )(own, other, gate_cols, up_cols)


def down_kernel(pieces, mine_ref, theirs_ref, *refs):
    down_refs, other_refs, back_ref = refs[:pieces], refs[pieces : 2 * pieces], refs[2 * pieces]
    quarter = back_ref.shape[2]
    shape = (CHIPS * ES * LAST, CHIPS * LAST)
    row = iota(shape, 0)
    source = iota(shape, 1)
    last = jnp.zeros((CHIPS * ES * LAST, quarter), F32)
    for q in range(ES):
        columns = slice(q * quarter, (q + 1) * quarter)
        total = jnp.zeros((mine_ref.shape[0], quarter), F32)
        for hidden_ref, weights in ((mine_ref, down_refs), (theirs_ref, other_refs)):
            block = jnp.concatenate([ref[:, columns] for ref in weights], axis=0)
            total = total + dot(hidden_ref[...], block)
        total = total.astype(BF16)
        for chip in range(CHIPS):
            back_ref[chip, q * MAIN : (q + 1) * MAIN, :] = total[chip * MAIN : (chip + 1) * MAIN]
        inside = row % (ES * LAST) - q * LAST
        pick = (inside >= 0) & (inside < LAST)
        pick = pick & (source == (row // (ES * LAST)) * LAST + inside)
        last = last + dot(pick.astype(BF16), total[CHIPS * MAIN :])
    for chip in range(CHIPS):
        rows = last[chip * ES * LAST : (chip + 1) * ES * LAST]
        back_ref[chip, ES * MAIN :, :] = rows.astype(BF16)


def down_product(mine, theirs, down, other_down):
    count, width = mine.shape
    features = down[0].shape[1]
    return pl.pallas_call(
        functools.partial(down_kernel, len(down)),
        out_shape=jax.ShapeDtypeStruct((CHIPS, ES * (MAIN + LAST), features // ES), BF16),
        compiler_params=pltpu.CompilerParams(vmem_limit_bytes=VMEM_LIMIT),
        cost_estimate=pl.CostEstimate(
            flops=4 * count * width * features,
            bytes_accessed=4 * width * features + 2 * count * features,
            transcendentals=0,
        ),
    )(mine, theirs, *down, *other_down)


def finish_kernel(current_ref, back_ref, ids_ref, scores_ref, out_ref):
    tokens, features = current_ref.shape
    quarter = features // ES
    ids_row = ids_ref[...]
    ids_column = to_column(ids_row)
    score = to_column(scores_ref[...])
    earlier = (ids_column == ids_row) & (iota((tokens, tokens), 1) < iota((tokens, tokens), 0))
    slot = jnp.sum(earlier.astype(jnp.int32), axis=1, keepdims=True)
    lane = iota((tokens, CHIPS * MAIN), 1)
    pick_main = (lane // (2 * MAIN) == ids_column) & (lane % MAIN == slot)
    pick_main = pick_main.astype(BF16)
    lane = iota((tokens, CHIPS * ES * LAST), 1)
    in_expert = (lane // (2 * ES * LAST) == ids_column) & (slot >= MAIN)
    in_block = lane % (ES * LAST)
    last = jnp.concatenate(
        [back_ref[ORDER.index(chip), ES * MAIN :, :].astype(F32) for chip in range(CHIPS)], axis=0
    ).astype(BF16)
    for q in range(ES):
        main = jnp.concatenate(
            [
                back_ref[ORDER.index(chip), q * MAIN : (q + 1) * MAIN, :]
                for chip in range(CHIPS)
            ],
            axis=0,
        )
        pick_last = in_expert & (in_block == q * LAST + slot - MAIN)
        moe = (dot(pick_main, main) + dot(pick_last.astype(BF16), last)) * score
        columns = slice(q * quarter, (q + 1) * quarter)
        out_ref[:, columns] = (current_ref[:, columns].astype(F32) + moe).astype(BF16)


def finish(current, back, ids_row, scores_row):
    tokens, features = current.shape
    return pl.pallas_call(
        finish_kernel,
        out_shape=jax.ShapeDtypeStruct((tokens, features), BF16),
        compiler_params=pltpu.CompilerParams(vmem_limit_bytes=VMEM_LIMIT),
        cost_estimate=pl.CostEstimate(
            flops=6 * tokens * EXPERTS * MAIN * features,
            bytes_accessed=8 * tokens * features,
            transcendentals=0,
        ),
    )(current, back, ids_row, scores_row)


def swap_cores(value):
    return lax.ppermute(value, "ep", [(i, i ^ 1) for i in range(EP)])


def from_behind(value, steps):
    count = lax.axis_size("section")
    return lax.ppermute(value, "section", [(i, (i + steps) % count) for i in range(count)])


def behind_other_core(value, steps):
    count = lax.axis_size("section")
    pairs = [
        (s * EP + i, ((s + steps) % count) * EP + (i ^ 1)) for s in range(count) for i in range(EP)
    ]
    return lax.ppermute(value, ("section", "ep"), pairs)


def exchange(blocks):
    same_core = [[2 * chip + core for chip in ORDER] for core in range(2)]
    return lax.all_to_all(
        blocks, "ep", split_axis=0, concat_axis=0, axis_index_groups=same_core, tiled=True
    )


def on_device(
    flight_a, flight_b, routes_a, routes_b, scores_a, scores_b, norm_gain, w_gate, w_up, w_down
):
    tokens = flight_a.shape[1]
    current_a, current_b = flight_a[0], flight_b[0]
    ids_a, ids_b = routes_a.reshape(1, tokens), routes_b.reshape(1, tokens)
    marks_a, marks_b = scores_a.reshape(1, tokens), scores_b.reshape(1, tokens)
    gate_cols, up_cols, down = w_gate[0], w_up[0], w_down[0]

    own_a = exchange(prepare(current_a, ids_a, norm_gain))
    send_b = prepare(current_b, ids_b, norm_gain)
    middle = down.shape[0] // 2
    upper = from_behind(down[:middle], -1)
    own_a, send_b, upper = lax.optimization_barrier((own_a, send_b, upper))
    own_b = exchange(send_b)

    lower = from_behind(down[middle:], -1)
    mine_a, give_a = hidden_units(own_a, swap_cores(own_a), gate_cols, up_cols)
    back_a = down_product(mine_a, swap_cores(give_a), [down], [swap_cores(down)])
    own_b, back_a, lower = lax.optimization_barrier((own_b, back_a, lower))

    returned_a = exchange(back_a)
    mine_b, give_b = hidden_units(own_b, swap_cores(own_b), gate_cols, up_cols)
    back_b = down_product(
        from_behind(mine_b, -1),
        behind_other_core(give_b, -1),
        [upper, lower],
        [swap_cores(upper), swap_cores(lower)],
    )
    moved_b, moved_ids, moved_marks = [
        from_behind(value, -1) for value in (current_b, ids_b, marks_b)
    ]

    marks_a, back_b = lax.optimization_barrier((marks_a, back_b))
    returned_b = exchange(back_b)
    updated_a = from_behind(finish(current_a, returned_a, ids_a, marks_a), 1)
    updated_b = finish(moved_b, returned_b, moved_ids, moved_marks)
    return (updated_a[None], updated_b[None])


def solution(mesh):
    placed = (
        P("section", "ep", None),
        P("section", "ep", None),
        P("section", None, "ep", None),
        P("section", None, "ep", None),
        P("section", None, "ep", None),
        P("section", None, "ep", None),
        P("section", None),
        P("section", None, "ep"),
        P("section", None, "ep"),
        P("section", "ep", None),
    )
    return jax.shard_map(
        on_device,
        mesh=mesh,
        in_specs=placed,
        out_specs=(P("section", "ep", None), P("section", "ep", None)),
        check_vma=False,
    )
```

```python
import functools

import jax
import jax.numpy as jnp
from jax import lax
from jax.experimental import pallas as pl
from jax.experimental.pallas import tpu as pltpu
from jax.sharding import PartitionSpec as P

ES = 4
EXPERTS = 8
EP = ES * EXPERTS
CHIPS = EP // 2
MAIN = 16
LAST = 2
EPSILON = 1e-06
F32 = jnp.float32
BF16 = jnp.bfloat16
VMEM_LIMIT = 48 * 1024 * 1024


def iota(shape, axis):
    return lax.broadcasted_iota(jnp.int32, shape, axis)


def to_column(row):
    count = row.shape[1]
    eye = iota((count, count), 0) == iota((count, count), 1)
    return jnp.sum(jnp.where(eye, row, jnp.zeros_like(row)), axis=1, keepdims=True)


def dot(left, right):
    return jnp.dot(left, right, preferred_element_type=F32)


def prepare_kernel(current_ref, ids_ref, gain_ref, send_ref):
    tokens, features = current_ref.shape
    quarter = features // ES
    ids_row = ids_ref[...]
    ids_column = to_column(ids_row)
    same = ids_column == ids_row
    earlier = same & (iota((tokens, tokens), 0) < iota((tokens, tokens), 1))
    slot_row = jnp.sum(earlier.astype(jnp.int32), axis=0, keepdims=True)
    main_row = jnp.where(slot_row < MAIN, ids_row * MAIN + slot_row, -1)
    last_row = jnp.where(slot_row < MAIN, -1, ids_row * (ES * LAST) + slot_row - MAIN)
    pick_main = (iota((EXPERTS * MAIN, tokens), 0) == main_row).astype(BF16)
    as_float = current_ref[...].astype(F32)
    inverse_rms = lax.rsqrt(jnp.mean(as_float * as_float, axis=-1, keepdims=True) + EPSILON)
    last = jnp.zeros((EXPERTS * ES * LAST, quarter), F32)
    for q in range(ES):
        columns = slice(q * quarter, (q + 1) * quarter)
        normed = (current_ref[:, columns].astype(F32) * inverse_rms * gain_ref[:, columns]).astype(
            BF16
        )
        main = dot(pick_main, normed).astype(BF16)
        for expert in range(EXPERTS):
            rows = main[expert * MAIN : (expert + 1) * MAIN]
            for chip in (2 * expert, 2 * expert + 1):
                send_ref[chip, q * MAIN : (q + 1) * MAIN, :] = rows
        place = jnp.where(last_row < 0, -1, last_row + q * LAST)
        pick_last = (iota((EXPERTS * ES * LAST, tokens), 0) == place).astype(BF16)
        last = last + dot(pick_last, normed)
    for expert in range(EXPERTS):
        rows = last[expert * ES * LAST : (expert + 1) * ES * LAST].astype(BF16)
        for chip in (2 * expert, 2 * expert + 1):
            send_ref[chip, ES * MAIN :, :] = rows


def prepare(current, ids_row, gain):
    tokens, features = current.shape
    quarter = features // ES
    return pl.pallas_call(
        prepare_kernel,
        out_shape=jax.ShapeDtypeStruct((CHIPS, ES * (MAIN + LAST), quarter), BF16),
        compiler_params=pltpu.CompilerParams(vmem_limit_bytes=VMEM_LIMIT),
        cost_estimate=pl.CostEstimate(
            flops=3 * tokens * tokens * features, bytes_accessed=8 * tokens * features, transcendentals=0
        ),
    )(current, ids_row, gain)


def hidden_kernel(own_ref, other_ref, gate_ref, up_ref, mine_ref, give_ref):
    quarter = own_ref.shape[2]
    count = CHIPS * (MAIN + LAST)
    for received, hidden_ref in ((own_ref, mine_ref), (other_ref, give_ref)):
        last = received[:, ES * MAIN :, :].astype(F32).reshape(CHIPS * ES * LAST, quarter).astype(BF16)
        gate = jnp.zeros((count, gate_ref.shape[1]), F32)
        up = jnp.zeros((count, up_ref.shape[1]), F32)
        shape = (CHIPS * LAST, CHIPS * ES * LAST)
        target = iota(shape, 0)
        source = (target // LAST) * (ES * LAST) + target % LAST
        for q in range(ES):
            main = received[:, q * MAIN : (q + 1) * MAIN, :].reshape(CHIPS * MAIN, quarter)
            pick = (iota(shape, 1) == source + q * LAST).astype(BF16)
            rows = jnp.concatenate([main, dot(pick, last).astype(BF16)], axis=0)
            gate = gate + dot(rows, gate_ref[q * quarter : (q + 1) * quarter, :])
            up = up + dot(rows, up_ref[q * quarter : (q + 1) * quarter, :])
        hidden_ref[...] = (jax.nn.silu(gate) * up).astype(BF16)


def hidden_units(own, other, gate_cols, up_cols):
    count = CHIPS * (MAIN + LAST)
    features, width = gate_cols.shape
    return pl.pallas_call(
        hidden_kernel,
        out_shape=[jax.ShapeDtypeStruct((count, width), BF16)] * 2,
        compiler_params=pltpu.CompilerParams(vmem_limit_bytes=VMEM_LIMIT),
        cost_estimate=pl.CostEstimate(
            flops=8 * count * features * width,
            bytes_accessed=4 * features * width + 4 * count * features,
            transcendentals=2 * count * width,
        ),
    )(own, other, gate_cols, up_cols)


def down_kernel(pieces, mine_ref, theirs_ref, *refs):
    down_refs, other_refs, back_ref = refs[:pieces], refs[pieces : 2 * pieces], refs[2 * pieces]
    quarter = back_ref.shape[2]
    shape = (CHIPS * ES * LAST, CHIPS * LAST)
    row = iota(shape, 0)
    source = iota(shape, 1)
    last = jnp.zeros((CHIPS * ES * LAST, quarter), F32)
    for q in range(ES):
        columns = slice(q * quarter, (q + 1) * quarter)
        total = jnp.zeros((mine_ref.shape[0], quarter), F32)
        for hidden_ref, weights in ((mine_ref, down_refs), (theirs_ref, other_refs)):
            block = jnp.concatenate([ref[:, columns] for ref in weights], axis=0)
            total = total + dot(hidden_ref[...], block)
        total = total.astype(BF16)
        for chip in range(CHIPS):
            back_ref[chip, q * MAIN : (q + 1) * MAIN, :] = total[chip * MAIN : (chip + 1) * MAIN]
        inside = row % (ES * LAST) - q * LAST
        pick = (inside >= 0) & (inside < LAST)
        pick = pick & (source == (row // (ES * LAST)) * LAST + inside)
        last = last + dot(pick.astype(BF16), total[CHIPS * MAIN :])
    for chip in range(CHIPS):
        rows = last[chip * ES * LAST : (chip + 1) * ES * LAST]
        back_ref[chip, ES * MAIN :, :] = rows.astype(BF16)


def down_product(mine, theirs, down, other_down):
    count, width = mine.shape
    features = down[0].shape[1]
    return pl.pallas_call(
        functools.partial(down_kernel, len(down)),
        out_shape=jax.ShapeDtypeStruct((CHIPS, ES * (MAIN + LAST), features // ES), BF16),
        compiler_params=pltpu.CompilerParams(vmem_limit_bytes=VMEM_LIMIT),
        cost_estimate=pl.CostEstimate(
            flops=4 * count * width * features,
            bytes_accessed=4 * width * features + 2 * count * features,
            transcendentals=0,
        ),
    )(mine, theirs, *down, *other_down)


def finish_kernel(current_ref, back_ref, ids_ref, scores_ref, out_ref):
    tokens, features = current_ref.shape
    quarter = features // ES
    ids_row = ids_ref[...]
    ids_column = to_column(ids_row)
    score = to_column(scores_ref[...])
    earlier = (ids_column == ids_row) & (iota((tokens, tokens), 1) < iota((tokens, tokens), 0))
    slot = jnp.sum(earlier.astype(jnp.int32), axis=1, keepdims=True)
    lane = iota((tokens, CHIPS * MAIN), 1)
    pick_main = (lane // (2 * MAIN) == ids_column) & (lane % MAIN == slot)
    pick_main = pick_main.astype(BF16)
    lane = iota((tokens, CHIPS * ES * LAST), 1)
    in_expert = (lane // (2 * ES * LAST) == ids_column) & (slot >= MAIN)
    in_block = lane % (ES * LAST)
    last = jnp.concatenate(
        [back_ref[chip, ES * MAIN :, :].astype(F32) for chip in range(CHIPS)], axis=0
    ).astype(BF16)
    for q in range(ES):
        main = jnp.concatenate(
            [back_ref[chip, q * MAIN : (q + 1) * MAIN, :] for chip in range(CHIPS)], axis=0
        )
        pick_last = in_expert & (in_block == q * LAST + slot - MAIN)
        moe = (dot(pick_main, main) + dot(pick_last.astype(BF16), last)) * score
        columns = slice(q * quarter, (q + 1) * quarter)
        out_ref[:, columns] = (current_ref[:, columns].astype(F32) + moe).astype(BF16)


def finish(current, back, ids_row, scores_row):
    tokens, features = current.shape
    return pl.pallas_call(
        finish_kernel,
        out_shape=jax.ShapeDtypeStruct((tokens, features), BF16),
        compiler_params=pltpu.CompilerParams(vmem_limit_bytes=VMEM_LIMIT),
        cost_estimate=pl.CostEstimate(
            flops=6 * tokens * EXPERTS * MAIN * features,
            bytes_accessed=8 * tokens * features,
            transcendentals=0,
        ),
    )(current, back, ids_row, scores_row)


def swap_cores(value):
    return lax.ppermute(value, "ep", [(i, i ^ 1) for i in range(EP)])


def from_behind(value, steps):
    count = lax.axis_size("section")
    return lax.ppermute(value, "section", [(i, (i + steps) % count) for i in range(count)])


def behind_other_core(value, steps):
    count = lax.axis_size("section")
    pairs = [
        (s * EP + i, ((s + steps) % count) * EP + (i ^ 1)) for s in range(count) for i in range(EP)
    ]
    return lax.ppermute(value, ("section", "ep"), pairs)


def exchange(blocks):
    same_core = [[2 * chip + core for chip in range(CHIPS)] for core in range(2)]
    return lax.all_to_all(
        blocks, "ep", split_axis=0, concat_axis=0, axis_index_groups=same_core, tiled=True
    )


def on_device(
    flight_a, flight_b, routes_a, routes_b, scores_a, scores_b, norm_gain, w_gate, w_up, w_down
):
    tokens = flight_a.shape[1]
    current_a, current_b = flight_a[0], flight_b[0]
    ids_a, ids_b = routes_a.reshape(1, tokens), routes_b.reshape(1, tokens)
    marks_a, marks_b = scores_a.reshape(1, tokens), scores_b.reshape(1, tokens)
    gate_cols, up_cols, down = w_gate[0], w_up[0], w_down[0]

    own_a = exchange(prepare(current_a, ids_a, norm_gain))
    send_b = prepare(current_b, ids_b, norm_gain)
    middle = down.shape[0] // 2
    upper = from_behind(down[:middle], -1)
    other_down = swap_cores(down)
    own_a, send_b, upper, other_down = lax.optimization_barrier((own_a, send_b, upper, other_down))
    own_b = exchange(send_b)

    lower = from_behind(down[middle:], -1)
    mine_a, give_a = hidden_units(own_a, swap_cores(own_a), gate_cols, up_cols)
    back_a = down_product(mine_a, swap_cores(give_a), [down], [other_down])
    own_b, back_a, lower = lax.optimization_barrier((own_b, back_a, lower))

    returned_a = exchange(back_a)
    mine_b, give_b = hidden_units(own_b, swap_cores(own_b), gate_cols, up_cols)
    back_b = down_product(
        from_behind(mine_b, -1),
        behind_other_core(give_b, -1),
        [upper, lower],
        [swap_cores(upper), swap_cores(lower)],
    )
    moved_b, moved_ids, moved_marks = [
        from_behind(value, -1) for value in (current_b, ids_b, marks_b)
    ]

    marks_a, back_b = lax.optimization_barrier((marks_a, back_b))
    returned_b = exchange(back_b)
    updated_a = from_behind(finish(current_a, returned_a, ids_a, marks_a), 1)
    updated_b = finish(moved_b, returned_b, moved_ids, moved_marks)
    return (updated_a[None], updated_b[None])


def solution(mesh):
    placed = (
        P("section", "ep", None),
        P("section", "ep", None),
        P("section", None, "ep", None),
        P("section", None, "ep", None),
        P("section", None, "ep", None),
        P("section", None, "ep", None),
        P("section", None),
        P("section", None, "ep"),
        P("section", None, "ep"),
        P("section", "ep", None),
    )
    return jax.shard_map(
        on_device,
        mesh=mesh,
        in_specs=placed,
        out_specs=(P("section", "ep", None), P("section", "ep", None)),
        check_vma=False,
    )
```

```python
import functools

import jax
import jax.numpy as jnp
from jax import lax
from jax.experimental import pallas as pl
from jax.experimental.pallas import tpu as pltpu
from jax.sharding import PartitionSpec as P

ES = 4
EXPERTS = 8
EP = ES * EXPERTS
CHIPS = EP // 2
MAIN = 16
LAST = 2
EPSILON = 1e-06
F32 = jnp.float32
BF16 = jnp.bfloat16
VMEM_LIMIT = 48 * 1024 * 1024
VMEM_WHOLE = 64 * 1024 * 1024 - 512 * 1024


def iota(shape, axis):
    return lax.broadcasted_iota(jnp.int32, shape, axis)


def to_column(row):
    count = row.shape[1]
    eye = iota((count, count), 0) == iota((count, count), 1)
    return jnp.sum(jnp.where(eye, row, jnp.zeros_like(row)), axis=1, keepdims=True)


def dot(left, right):
    return jnp.dot(left, right, preferred_element_type=F32)


def prepare_kernel(current_hbm, ids_hbm, gain_hbm, send_ref, current_ref, ids_ref, gain_ref, ready):
    loads = [
        pltpu.make_async_copy(source, target, ready.at[place])
        for place, (source, target) in enumerate(
            ((ids_hbm, ids_ref), (current_hbm, current_ref), (gain_hbm, gain_ref))
        )
    ]
    for load in loads:
        load.start()
    tokens, features = current_ref.shape
    quarter = features // ES
    loads[0].wait()
    ids_row = ids_ref[...]
    ids_column = to_column(ids_row)
    same = ids_column == ids_row
    earlier = same & (iota((tokens, tokens), 0) < iota((tokens, tokens), 1))
    slot_row = jnp.sum(earlier.astype(jnp.int32), axis=0, keepdims=True)
    main_row = jnp.where(slot_row < MAIN, ids_row * MAIN + slot_row, -1)
    last_row = jnp.where(slot_row < MAIN, -1, ids_row * (ES * LAST) + slot_row - MAIN)
    pick_main = (iota((EXPERTS * MAIN, tokens), 0) == main_row).astype(BF16)
    loads[1].wait()
    loads[2].wait()
    as_float = current_ref[...].astype(F32)
    inverse_rms = lax.rsqrt(jnp.mean(as_float * as_float, axis=-1, keepdims=True) + EPSILON)
    last = jnp.zeros((EXPERTS * ES * LAST, quarter), F32)
    for q in range(ES):
        columns = slice(q * quarter, (q + 1) * quarter)
        normed = (current_ref[:, columns].astype(F32) * inverse_rms * gain_ref[:, columns]).astype(
            BF16
        )
        main = dot(pick_main, normed).astype(BF16)
        for expert in range(EXPERTS):
            rows = main[expert * MAIN : (expert + 1) * MAIN]
            for chip in (2 * expert, 2 * expert + 1):
                send_ref[chip, q * MAIN : (q + 1) * MAIN, :] = rows
        place = jnp.where(last_row < 0, -1, last_row + q * LAST)
        pick_last = (iota((EXPERTS * ES * LAST, tokens), 0) == place).astype(BF16)
        last = last + dot(pick_last, normed)
    for expert in range(EXPERTS):
        rows = last[expert * ES * LAST : (expert + 1) * ES * LAST].astype(BF16)
        for chip in (2 * expert, 2 * expert + 1):
            send_ref[chip, ES * MAIN :, :] = rows


def prepare(current, ids_row, gain):
    tokens, features = current.shape
    quarter = features // ES
    return pl.pallas_call(
        prepare_kernel,
        out_shape=jax.ShapeDtypeStruct((CHIPS, ES * (MAIN + LAST), quarter), BF16),
        in_specs=[pl.BlockSpec(memory_space=pltpu.HBM)] * 3,
        scratch_shapes=[
            pltpu.VMEM(current.shape, current.dtype),
            pltpu.VMEM(ids_row.shape, ids_row.dtype),
            pltpu.VMEM(gain.shape, gain.dtype),
            pltpu.SemaphoreType.DMA((3,)),
        ],
        compiler_params=pltpu.CompilerParams(vmem_limit_bytes=VMEM_WHOLE),
        cost_estimate=pl.CostEstimate(
            flops=3 * tokens * tokens * features, bytes_accessed=8 * tokens * features, transcendentals=0
        ),
    )(current, ids_row, gain)


def hidden_kernel(own_ref, other_ref, gate_ref, up_ref, mine_ref, give_ref):
    quarter = own_ref.shape[2]
    count = CHIPS * (MAIN + LAST)
    for received, hidden_ref in ((own_ref, mine_ref), (other_ref, give_ref)):
        last = received[:, ES * MAIN :, :].astype(F32).reshape(CHIPS * ES * LAST, quarter).astype(BF16)
        gate = jnp.zeros((count, gate_ref.shape[1]), F32)
        up = jnp.zeros((count, up_ref.shape[1]), F32)
        shape = (CHIPS * LAST, CHIPS * ES * LAST)
        target = iota(shape, 0)
        source = (target // LAST) * (ES * LAST) + target % LAST
        for q in range(ES):
            main = received[:, q * MAIN : (q + 1) * MAIN, :].reshape(CHIPS * MAIN, quarter)
            pick = (iota(shape, 1) == source + q * LAST).astype(BF16)
            rows = jnp.concatenate([main, dot(pick, last).astype(BF16)], axis=0)
            gate = gate + dot(rows, gate_ref[q * quarter : (q + 1) * quarter, :])
            up = up + dot(rows, up_ref[q * quarter : (q + 1) * quarter, :])
        hidden_ref[...] = (jax.nn.silu(gate) * up).astype(BF16)


def hidden_units(own, other, gate_cols, up_cols):
    count = CHIPS * (MAIN + LAST)
    features, width = gate_cols.shape
    return pl.pallas_call(
        hidden_kernel,
        out_shape=[jax.ShapeDtypeStruct((count, width), BF16)] * 2,
        compiler_params=pltpu.CompilerParams(vmem_limit_bytes=VMEM_LIMIT),
        cost_estimate=pl.CostEstimate(
            flops=8 * count * features * width,
            bytes_accessed=4 * features * width + 4 * count * features,
            transcendentals=2 * count * width,
        ),
    )(own, other, gate_cols, up_cols)


def down_kernel(pieces, mine_ref, theirs_ref, *refs):
    down_refs, other_refs, back_ref = refs[:pieces], refs[pieces : 2 * pieces], refs[2 * pieces]
    quarter = back_ref.shape[2]
    shape = (CHIPS * ES * LAST, CHIPS * LAST)
    row = iota(shape, 0)
    source = iota(shape, 1)
    last = jnp.zeros((CHIPS * ES * LAST, quarter), F32)
    for q in range(ES):
        columns = slice(q * quarter, (q + 1) * quarter)
        total = jnp.zeros((mine_ref.shape[0], quarter), F32)
        for hidden_ref, weights in ((mine_ref, down_refs), (theirs_ref, other_refs)):
            block = jnp.concatenate([ref[:, columns] for ref in weights], axis=0)
            total = total + dot(hidden_ref[...], block)
        total = total.astype(BF16)
        for chip in range(CHIPS):
            back_ref[chip, q * MAIN : (q + 1) * MAIN, :] = total[chip * MAIN : (chip + 1) * MAIN]
        inside = row % (ES * LAST) - q * LAST
        pick = (inside >= 0) & (inside < LAST)
        pick = pick & (source == (row // (ES * LAST)) * LAST + inside)
        last = last + dot(pick.astype(BF16), total[CHIPS * MAIN :])
    for chip in range(CHIPS):
        rows = last[chip * ES * LAST : (chip + 1) * ES * LAST]
        back_ref[chip, ES * MAIN :, :] = rows.astype(BF16)


def down_product(mine, theirs, down, other_down):
    count, width = mine.shape
    features = down[0].shape[1]
    return pl.pallas_call(
        functools.partial(down_kernel, len(down)),
        out_shape=jax.ShapeDtypeStruct((CHIPS, ES * (MAIN + LAST), features // ES), BF16),
        compiler_params=pltpu.CompilerParams(vmem_limit_bytes=VMEM_LIMIT),
        cost_estimate=pl.CostEstimate(
            flops=4 * count * width * features,
            bytes_accessed=4 * width * features + 2 * count * features,
            transcendentals=0,
        ),
    )(mine, theirs, *down, *other_down)


def finish_kernel(current_ref, back_ref, ids_ref, scores_ref, out_ref):
    tokens, features = current_ref.shape
    quarter = features // ES
    ids_row = ids_ref[...]
    ids_column = to_column(ids_row)
    score = to_column(scores_ref[...])
    earlier = (ids_column == ids_row) & (iota((tokens, tokens), 1) < iota((tokens, tokens), 0))
    slot = jnp.sum(earlier.astype(jnp.int32), axis=1, keepdims=True)
    lane = iota((tokens, CHIPS * MAIN), 1)
    pick_main = (lane // (2 * MAIN) == ids_column) & (lane % MAIN == slot)
    pick_main = pick_main.astype(BF16)
    lane = iota((tokens, CHIPS * ES * LAST), 1)
    in_expert = (lane // (2 * ES * LAST) == ids_column) & (slot >= MAIN)
    in_block = lane % (ES * LAST)
    last = jnp.concatenate(
        [back_ref[chip, ES * MAIN :, :].astype(F32) for chip in range(CHIPS)], axis=0
    ).astype(BF16)
    for q in range(ES):
        main = jnp.concatenate(
            [back_ref[chip, q * MAIN : (q + 1) * MAIN, :] for chip in range(CHIPS)], axis=0
        )
        pick_last = in_expert & (in_block == q * LAST + slot - MAIN)
        moe = (dot(pick_main, main) + dot(pick_last.astype(BF16), last)) * score
        columns = slice(q * quarter, (q + 1) * quarter)
        out_ref[:, columns] = (current_ref[:, columns].astype(F32) + moe).astype(BF16)


def finish(current, back, ids_row, scores_row):
    tokens, features = current.shape
    return pl.pallas_call(
        finish_kernel,
        out_shape=jax.ShapeDtypeStruct((tokens, features), BF16),
        compiler_params=pltpu.CompilerParams(vmem_limit_bytes=VMEM_LIMIT),
        cost_estimate=pl.CostEstimate(
            flops=6 * tokens * EXPERTS * MAIN * features,
            bytes_accessed=8 * tokens * features,
            transcendentals=0,
        ),
    )(current, back, ids_row, scores_row)


def settle_kernel(value_ref, out_ref):
    out_ref[...] = value_ref[...]


def settle(value):
    return pl.pallas_call(
        settle_kernel,
        out_shape=jax.ShapeDtypeStruct(value.shape, value.dtype),
        compiler_params=pltpu.CompilerParams(vmem_limit_bytes=VMEM_LIMIT),
        cost_estimate=pl.CostEstimate(flops=0, bytes_accessed=4 * value.size, transcendentals=0),
    )(value)


def swap_cores(value):
    return lax.ppermute(value, "ep", [(i, i ^ 1) for i in range(EP)])


def from_behind(value, steps):
    count = lax.axis_size("section")
    return lax.ppermute(value, "section", [(i, (i + steps) % count) for i in range(count)])


def behind_other_core(value, steps):
    count = lax.axis_size("section")
    pairs = [
        (s * EP + i, ((s + steps) % count) * EP + (i ^ 1)) for s in range(count) for i in range(EP)
    ]
    return lax.ppermute(value, ("section", "ep"), pairs)


def exchange(blocks):
    same_core = [[2 * chip + core for chip in range(CHIPS)] for core in range(2)]
    return lax.all_to_all(
        blocks, "ep", split_axis=0, concat_axis=0, axis_index_groups=same_core, tiled=True
    )


def on_device(
    flight_a, flight_b, routes_a, routes_b, scores_a, scores_b, norm_gain, w_gate, w_up, w_down
):
    tokens = flight_a.shape[1]
    current_a, current_b = flight_a[0], flight_b[0]
    ids_a, ids_b = routes_a.reshape(1, tokens), routes_b.reshape(1, tokens)
    marks_a, marks_b = scores_a.reshape(1, tokens), scores_b.reshape(1, tokens)
    gate_cols, up_cols, down = w_gate[0], w_up[0], w_down[0]

    own_a = exchange(prepare(current_a, ids_a, norm_gain))
    other_down = swap_cores(down)
    staged_b, other_down = lax.optimization_barrier((current_b, other_down))
    send_b = prepare(staged_b, ids_b, norm_gain)
    upper = from_behind(down[:96], -1)
    own_a, send_b, upper = lax.optimization_barrier((own_a, send_b, upper))
    own_b = exchange(send_b)

    middle = from_behind(down[96:208], -1)
    mine_a, give_a = hidden_units(own_a, swap_cores(own_a), gate_cols, up_cols)
    back_a = down_product(mine_a, swap_cores(give_a), [down], [other_down])
    own_b, back_a, middle = lax.optimization_barrier((own_b, back_a, middle))

    returned_a = exchange(back_a)
    lower = from_behind(down[208:], -1)
    mine_b, give_b = hidden_units(own_b, swap_cores(own_b), gate_cols, up_cols)
    mine_b, give_b, lower = lax.optimization_barrier((mine_b, give_b, lower))
    moved_down = [upper, middle, lower]
    back_b = down_product(
        from_behind(mine_b, -1),
        behind_other_core(give_b, -1),
        moved_down,
        [swap_cores(piece) for piece in moved_down],
    )
    moved_b, moved_ids, moved_marks = [
        from_behind(value, -1) for value in (current_b, ids_b, marks_b)
    ]

    marks_a, back_b = lax.optimization_barrier((marks_a, back_b))
    returned_b = exchange(back_b)
    updated_a = settle(from_behind(finish(current_a, returned_a, ids_a, marks_a), 1))
    updated_b = finish(moved_b, returned_b, moved_ids, moved_marks)
    return (updated_a[None], updated_b[None])


def solution(mesh):
    placed = (
        P("section", "ep", None),
        P("section", "ep", None),
        P("section", None, "ep", None),
        P("section", None, "ep", None),
        P("section", None, "ep", None),
        P("section", None, "ep", None),
        P("section", None),
        P("section", None, "ep"),
        P("section", None, "ep"),
        P("section", "ep", None),
    )
    return jax.shard_map(
        on_device,
        mesh=mesh,
        in_specs=placed,
        out_specs=(P("section", "ep", None), P("section", "ep", None)),
        check_vma=False,
    )
```

```python
import functools

import jax
import jax.numpy as jnp
from jax import lax
from jax.experimental import pallas as pl
from jax.experimental.pallas import tpu as pltpu
from jax.sharding import PartitionSpec as P

ES = 4
EXPERTS = 8
EP = ES * EXPERTS
CHIPS = EP // 2
MAIN = 16
LAST = 2
EPSILON = 1e-06
F32 = jnp.float32
BF16 = jnp.bfloat16
VMEM_LIMIT = 48 * 1024 * 1024
VMEM_WHOLE = 64 * 1024 * 1024 - 512 * 1024


def iota(shape, axis):
    return lax.broadcasted_iota(jnp.int32, shape, axis)


def to_column(row):
    count = row.shape[1]
    eye = iota((count, count), 0) == iota((count, count), 1)
    return jnp.sum(jnp.where(eye, row, jnp.zeros_like(row)), axis=1, keepdims=True)


def dot(left, right):
    return jnp.dot(left, right, preferred_element_type=F32)


def prepare_kernel(current_hbm, ids_hbm, gain_hbm, send_ref, current_ref, ids_ref, gain_ref, ready):
    loads = [
        pltpu.make_async_copy(source, target, ready.at[place])
        for place, (source, target) in enumerate(
            ((ids_hbm, ids_ref), (current_hbm, current_ref), (gain_hbm, gain_ref))
        )
    ]
    for load in loads:
        load.start()
    tokens, features = current_ref.shape
    quarter = features // ES
    loads[0].wait()
    ids_row = ids_ref[...]
    ids_column = to_column(ids_row)
    same = ids_column == ids_row
    earlier = same & (iota((tokens, tokens), 0) < iota((tokens, tokens), 1))
    slot_row = jnp.sum(earlier.astype(jnp.int32), axis=0, keepdims=True)
    main_row = jnp.where(slot_row < MAIN, ids_row * MAIN + slot_row, -1)
    last_row = jnp.where(slot_row < MAIN, -1, ids_row * (ES * LAST) + slot_row - MAIN)
    pick_main = (iota((EXPERTS * MAIN, tokens), 0) == main_row).astype(BF16)
    loads[1].wait()
    loads[2].wait()
    as_float = current_ref[...].astype(F32)
    inverse_rms = lax.rsqrt(jnp.mean(as_float * as_float, axis=-1, keepdims=True) + EPSILON)
    last = jnp.zeros((EXPERTS * ES * LAST, quarter), F32)
    for q in range(ES):
        columns = slice(q * quarter, (q + 1) * quarter)
        normed = (current_ref[:, columns].astype(F32) * inverse_rms * gain_ref[:, columns]).astype(
            BF16
        )
        main = dot(pick_main, normed).astype(BF16)
        for expert in range(EXPERTS):
            rows = main[expert * MAIN : (expert + 1) * MAIN]
            for chip in (2 * expert, 2 * expert + 1):
                send_ref[chip, q * MAIN : (q + 1) * MAIN, :] = rows
        place = jnp.where(last_row < 0, -1, last_row + q * LAST)
        pick_last = (iota((EXPERTS * ES * LAST, tokens), 0) == place).astype(BF16)
        last = last + dot(pick_last, normed)
    for expert in range(EXPERTS):
        rows = last[expert * ES * LAST : (expert + 1) * ES * LAST].astype(BF16)
        for chip in (2 * expert, 2 * expert + 1):
            send_ref[chip, ES * MAIN :, :] = rows


def prepare(current, ids_row, gain):
    tokens, features = current.shape
    quarter = features // ES
    return pl.pallas_call(
        prepare_kernel,
        out_shape=jax.ShapeDtypeStruct((CHIPS, ES * (MAIN + LAST), quarter), BF16),
        in_specs=[pl.BlockSpec(memory_space=pltpu.HBM)] * 3,
        scratch_shapes=[
            pltpu.VMEM(current.shape, current.dtype),
            pltpu.VMEM(ids_row.shape, ids_row.dtype),
            pltpu.VMEM(gain.shape, gain.dtype),
            pltpu.SemaphoreType.DMA((3,)),
        ],
        compiler_params=pltpu.CompilerParams(vmem_limit_bytes=VMEM_WHOLE),
        cost_estimate=pl.CostEstimate(
            flops=3 * tokens * tokens * features, bytes_accessed=8 * tokens * features, transcendentals=0
        ),
    )(current, ids_row, gain)


def hidden_kernel(
    received_hbm, gate_hbm, up_hbm, hidden_ref, received_ref, gate_ref, up_ref, ready
):
    quarter = received_ref.shape[2]
    count = CHIPS * (MAIN + LAST)
    loads = [pltpu.make_async_copy(received_hbm, received_ref, ready.at[2 * ES])]
    for q in range(ES):
        part = pl.ds(q * quarter, quarter)
        for side, (source, target) in enumerate(((gate_hbm, gate_ref), (up_hbm, up_ref))):
            loads.append(
                pltpu.make_async_copy(source.at[part, :], target.at[part, :], ready.at[2 * q + side])
            )
    for load in loads:
        load.start()
    gate = jnp.zeros((count, gate_ref.shape[1]), F32)
    up = jnp.zeros((count, up_ref.shape[1]), F32)
    shape = (CHIPS * LAST, CHIPS * ES * LAST)
    target = iota(shape, 0)
    source = (target // LAST) * (ES * LAST) + target % LAST
    loads[0].wait()
    last = received_ref[:, ES * MAIN :, :].astype(F32)
    last = last.reshape(CHIPS * ES * LAST, quarter).astype(BF16)
    for q in range(ES):
        main = received_ref[:, q * MAIN : (q + 1) * MAIN, :].reshape(CHIPS * MAIN, quarter)
        pick = (iota(shape, 1) == source + q * LAST).astype(BF16)
        rows = jnp.concatenate([main, dot(pick, last).astype(BF16)], axis=0)
        loads[1 + 2 * q].wait()
        gate = gate + dot(rows, gate_ref[q * quarter : (q + 1) * quarter, :])
        loads[2 + 2 * q].wait()
        up = up + dot(rows, up_ref[q * quarter : (q + 1) * quarter, :])
    hidden_ref[...] = (jax.nn.silu(gate) * up).astype(BF16)


def hidden_units(received, gate_cols, up_cols):
    count = CHIPS * (MAIN + LAST)
    features, width = gate_cols.shape
    return pl.pallas_call(
        hidden_kernel,
        out_shape=jax.ShapeDtypeStruct((count, width), BF16),
        in_specs=[pl.BlockSpec(memory_space=pltpu.HBM)] * 3,
        scratch_shapes=[
            pltpu.VMEM(received.shape, received.dtype),
            pltpu.VMEM(gate_cols.shape, gate_cols.dtype),
            pltpu.VMEM(up_cols.shape, up_cols.dtype),
            pltpu.SemaphoreType.DMA((2 * ES + 1,)),
        ],
        compiler_params=pltpu.CompilerParams(vmem_limit_bytes=VMEM_WHOLE),
        cost_estimate=pl.CostEstimate(
            flops=4 * count * features * width,
            bytes_accessed=4 * features * width + 2 * count * features,
            transcendentals=count * width,
        ),
    )(received, gate_cols, up_cols)


def down_kernel(pieces, mine_ref, theirs_ref, *refs):
    down_refs, other_refs, back_ref = refs[:pieces], refs[pieces : 2 * pieces], refs[2 * pieces]
    quarter = back_ref.shape[2]
    shape = (CHIPS * ES * LAST, CHIPS * LAST)
    row = iota(shape, 0)
    source = iota(shape, 1)
    last = jnp.zeros((CHIPS * ES * LAST, quarter), F32)
    for q in range(ES):
        columns = slice(q * quarter, (q + 1) * quarter)
        total = jnp.zeros((mine_ref.shape[0], quarter), F32)
        for hidden_ref, weights in ((mine_ref, down_refs), (theirs_ref, other_refs)):
            block = jnp.concatenate([ref[:, columns] for ref in weights], axis=0)
            total = total + dot(hidden_ref[...], block)
        total = total.astype(BF16)
        for chip in range(CHIPS):
            back_ref[chip, q * MAIN : (q + 1) * MAIN, :] = total[chip * MAIN : (chip + 1) * MAIN]
        inside = row % (ES * LAST) - q * LAST
        pick = (inside >= 0) & (inside < LAST)
        pick = pick & (source == (row // (ES * LAST)) * LAST + inside)
        last = last + dot(pick.astype(BF16), total[CHIPS * MAIN :])
    for chip in range(CHIPS):
        rows = last[chip * ES * LAST : (chip + 1) * ES * LAST]
        back_ref[chip, ES * MAIN :, :] = rows.astype(BF16)


def down_product(mine, theirs, down, other_down):
    count, width = mine.shape
    features = down[0].shape[1]
    return pl.pallas_call(
        functools.partial(down_kernel, len(down)),
        out_shape=jax.ShapeDtypeStruct((CHIPS, ES * (MAIN + LAST), features // ES), BF16),
        compiler_params=pltpu.CompilerParams(vmem_limit_bytes=VMEM_LIMIT),
        cost_estimate=pl.CostEstimate(
            flops=4 * count * width * features,
            bytes_accessed=4 * width * features + 2 * count * features,
            transcendentals=0,
        ),
    )(mine, theirs, *down, *other_down)


def finish_kernel(
    current_hbm, back_hbm, ids_ref, scores_ref, out_hbm, current_ref, back_ref, out_ref, ready, done
):
    loads = [
        pltpu.make_async_copy(back_hbm, back_ref, ready.at[0]),
        pltpu.make_async_copy(current_hbm, current_ref, ready.at[1]),
    ]
    for load in loads:
        load.start()
    tokens, features = current_ref.shape
    quarter = features // ES
    ids_row = ids_ref[...]
    ids_column = to_column(ids_row)
    score = to_column(scores_ref[...])
    earlier = (ids_column == ids_row) & (iota((tokens, tokens), 1) < iota((tokens, tokens), 0))
    slot = jnp.sum(earlier.astype(jnp.int32), axis=1, keepdims=True)
    lane = iota((tokens, CHIPS * MAIN), 1)
    pick_main = (lane // (2 * MAIN) == ids_column) & (lane % MAIN == slot)
    pick_main = pick_main.astype(BF16)
    lane = iota((tokens, CHIPS * ES * LAST), 1)
    in_expert = (lane // (2 * ES * LAST) == ids_column) & (slot >= MAIN)
    in_block = lane % (ES * LAST)
    loads[0].wait()
    last = jnp.concatenate(
        [back_ref[chip, ES * MAIN :, :].astype(F32) for chip in range(CHIPS)], axis=0
    ).astype(BF16)
    loads[1].wait()
    stores = []
    for q in range(ES):
        main = jnp.concatenate(
            [back_ref[chip, q * MAIN : (q + 1) * MAIN, :] for chip in range(CHIPS)], axis=0
        )
        pick_last = in_expert & (in_block == q * LAST + slot - MAIN)
        moe = (dot(pick_main, main) + dot(pick_last.astype(BF16), last)) * score
        columns = slice(q * quarter, (q + 1) * quarter)
        out_ref[:, columns] = (current_ref[:, columns].astype(F32) + moe).astype(BF16)
        part = pl.ds(q * quarter, quarter)
        stores.append(pltpu.make_async_copy(out_ref.at[:, part], out_hbm.at[:, part], done.at[q]))
        stores[q].start()
    for store in stores:
        store.wait()


def finish(current, back, ids_row, scores_row):
    tokens, features = current.shape
    return pl.pallas_call(
        finish_kernel,
        out_shape=jax.ShapeDtypeStruct((tokens, features), BF16),
        in_specs=[pl.BlockSpec(memory_space=pltpu.HBM)] * 2
        + [pl.BlockSpec(memory_space=pltpu.VMEM)] * 2,
        out_specs=pl.BlockSpec(memory_space=pltpu.HBM),
        scratch_shapes=[
            pltpu.VMEM(current.shape, BF16),
            pltpu.VMEM(back.shape, BF16),
            pltpu.VMEM(current.shape, BF16),
            pltpu.SemaphoreType.DMA((2,)),
            pltpu.SemaphoreType.DMA((ES,)),
        ],
        compiler_params=pltpu.CompilerParams(vmem_limit_bytes=VMEM_WHOLE),
        cost_estimate=pl.CostEstimate(
            flops=6 * tokens * EXPERTS * MAIN * features,
            bytes_accessed=8 * tokens * features,
            transcendentals=0,
        ),
    )(current, back, ids_row, scores_row)


def settle_kernel(value_ref, out_ref):
    out_ref[...] = value_ref[...]


def settle(value):
    return pl.pallas_call(
        settle_kernel,
        out_shape=jax.ShapeDtypeStruct(value.shape, value.dtype),
        compiler_params=pltpu.CompilerParams(vmem_limit_bytes=VMEM_LIMIT),
        cost_estimate=pl.CostEstimate(flops=0, bytes_accessed=4 * value.size, transcendentals=0),
    )(value)


def swap_cores(value):
    return lax.ppermute(value, "ep", [(i, i ^ 1) for i in range(EP)])


def from_behind(value, steps):
    count = lax.axis_size("section")
    return lax.ppermute(value, "section", [(i, (i + steps) % count) for i in range(count)])


def behind_other_core(value, steps):
    count = lax.axis_size("section")
    pairs = [
        (s * EP + i, ((s + steps) % count) * EP + (i ^ 1)) for s in range(count) for i in range(EP)
    ]
    return lax.ppermute(value, ("section", "ep"), pairs)


def exchange(blocks):
    same_core = [[2 * chip + core for chip in range(CHIPS)] for core in range(2)]
    return lax.all_to_all(
        blocks, "ep", split_axis=0, concat_axis=0, axis_index_groups=same_core, tiled=True
    )


def on_device(
    flight_a, flight_b, routes_a, routes_b, scores_a, scores_b, norm_gain, w_gate, w_up, w_down
):
    tokens = flight_a.shape[1]
    current_a, current_b = flight_a[0], flight_b[0]
    ids_a, ids_b = routes_a.reshape(1, tokens), routes_b.reshape(1, tokens)
    marks_a, marks_b = scores_a.reshape(1, tokens), scores_b.reshape(1, tokens)
    gate_cols, up_cols, down = w_gate[0], w_up[0], w_down[0]

    own_a = exchange(prepare(current_a, ids_a, norm_gain))
    other_down = swap_cores(down)
    staged_b, other_down = lax.optimization_barrier((current_b, other_down))
    send_b = prepare(staged_b, ids_b, norm_gain)
    middle = down.shape[0] // 2
    upper = from_behind(down[:middle], -1)
    own_a, send_b, upper = lax.optimization_barrier((own_a, send_b, upper))
    own_b = exchange(send_b)

    lower = from_behind(down[middle:], -1)
    mine_a = hidden_units(own_a, gate_cols, up_cols)
    give_a = hidden_units(swap_cores(own_a), gate_cols, up_cols)
    back_a = down_product(mine_a, swap_cores(give_a), [down], [other_down])
    own_b, back_a, lower = lax.optimization_barrier((own_b, back_a, lower))

    returned_a = exchange(back_a)
    mine_b = hidden_units(own_b, gate_cols, up_cols)
    give_b = hidden_units(swap_cores(own_b), gate_cols, up_cols)
    moved_down = [upper, lower]
    back_b = down_product(
        from_behind(mine_b, -1),
        behind_other_core(give_b, -1),
        moved_down,
        [swap_cores(piece) for piece in moved_down],
    )
    moved_b, moved_ids, moved_marks = [
        from_behind(value, -1) for value in (current_b, ids_b, marks_b)
    ]

    marks_a, back_b = lax.optimization_barrier((marks_a, back_b))
    returned_b = exchange(back_b)
    updated_a = settle(from_behind(finish(current_a, returned_a, ids_a, marks_a), 1))
    updated_b = finish(moved_b, returned_b, moved_ids, moved_marks)
    return (updated_a[None], updated_b[None])


def solution(mesh):
    placed = (
        P("section", "ep", None),
        P("section", "ep", None),
        P("section", None, "ep", None),
        P("section", None, "ep", None),
        P("section", None, "ep", None),
        P("section", None, "ep", None),
        P("section", None),
        P("section", None, "ep"),
        P("section", None, "ep"),
        P("section", "ep", None),
    )
    return jax.shard_map(
        on_device,
        mesh=mesh,
        in_specs=placed,
        out_specs=(P("section", "ep", None), P("section", "ep", None)),
        check_vma=False,
    )
```

```python
import functools

import jax
import jax.numpy as jnp
from jax import lax
from jax.experimental import pallas as pl
from jax.experimental.pallas import tpu as pltpu
from jax.sharding import PartitionSpec as P

ES = 4
EXPERTS = 8
EP = ES * EXPERTS
CHIPS = EP // 2
MAIN = 16
LAST = 2
EPSILON = 1e-06
F32 = jnp.float32
BF16 = jnp.bfloat16
VMEM_LIMIT = 20 * 1024 * 1024
VMEM_WHOLE = 64 * 1024 * 1024 - 512 * 1024


def iota(shape, axis):
    return lax.broadcasted_iota(jnp.int32, shape, axis)


def to_column(row):
    count = row.shape[1]
    eye = iota((count, count), 0) == iota((count, count), 1)
    return jnp.sum(jnp.where(eye, row, jnp.zeros_like(row)), axis=1, keepdims=True)


def dot(left, right):
    return jnp.dot(left, right, preferred_element_type=F32)


def prepare_kernel(current_hbm, ids_hbm, gain_hbm, send_ref, current_ref, ids_ref, gain_ref, ready):
    loads = [
        pltpu.make_async_copy(source, target, ready.at[place])
        for place, (source, target) in enumerate(
            ((ids_hbm, ids_ref), (current_hbm, current_ref), (gain_hbm, gain_ref))
        )
    ]
    for load in loads:
        load.start()
    tokens, features = current_ref.shape
    quarter = features // ES
    loads[0].wait()
    ids_row = ids_ref[...]
    ids_column = to_column(ids_row)
    same = ids_column == ids_row
    earlier = same & (iota((tokens, tokens), 0) < iota((tokens, tokens), 1))
    slot_row = jnp.sum(earlier.astype(jnp.int32), axis=0, keepdims=True)
    main_row = jnp.where(slot_row < MAIN, ids_row * MAIN + slot_row, -1)
    last_row = jnp.where(slot_row < MAIN, -1, ids_row * (ES * LAST) + slot_row - MAIN)
    pick_main = (iota((EXPERTS * MAIN, tokens), 0) == main_row).astype(BF16)
    loads[1].wait()
    loads[2].wait()
    as_float = current_ref[...].astype(F32)
    inverse_rms = lax.rsqrt(jnp.mean(as_float * as_float, axis=-1, keepdims=True) + EPSILON)
    last = jnp.zeros((EXPERTS * ES * LAST, quarter), F32)
    for q in range(ES):
        columns = slice(q * quarter, (q + 1) * quarter)
        normed = (current_ref[:, columns].astype(F32) * inverse_rms * gain_ref[:, columns]).astype(
            BF16
        )
        main = dot(pick_main, normed).astype(BF16)
        for expert in range(EXPERTS):
            rows = main[expert * MAIN : (expert + 1) * MAIN]
            for chip in (2 * expert, 2 * expert + 1):
                send_ref[chip, q * MAIN : (q + 1) * MAIN, :] = rows
        place = jnp.where(last_row < 0, -1, last_row + q * LAST)
        pick_last = (iota((EXPERTS * ES * LAST, tokens), 0) == place).astype(BF16)
        last = last + dot(pick_last, normed)
    for expert in range(EXPERTS):
        rows = last[expert * ES * LAST : (expert + 1) * ES * LAST].astype(BF16)
        for chip in (2 * expert, 2 * expert + 1):
            send_ref[chip, ES * MAIN :, :] = rows


def prepare(current, ids_row, gain, vmem):
    tokens, features = current.shape
    quarter = features // ES
    return pl.pallas_call(
        prepare_kernel,
        out_shape=jax.ShapeDtypeStruct((CHIPS, ES * (MAIN + LAST), quarter), BF16),
        in_specs=[pl.BlockSpec(memory_space=pltpu.HBM)] * 3,
        scratch_shapes=[
            pltpu.VMEM(current.shape, current.dtype),
            pltpu.VMEM(ids_row.shape, ids_row.dtype),
            pltpu.VMEM(gain.shape, gain.dtype),
            pltpu.SemaphoreType.DMA((3,)),
        ],
        compiler_params=pltpu.CompilerParams(vmem_limit_bytes=vmem),
        cost_estimate=pl.CostEstimate(
            flops=3 * tokens * tokens * features, bytes_accessed=8 * tokens * features, transcendentals=0
        ),
    )(current, ids_row, gain)


def hidden_kernel(received_ref, gate_ref, up_ref, hidden_ref):
    quarter = received_ref.shape[2]
    count = CHIPS * (MAIN + LAST)
    gate = jnp.zeros((count, gate_ref.shape[1]), F32)
    up = jnp.zeros((count, up_ref.shape[1]), F32)
    shape = (CHIPS * LAST, CHIPS * ES * LAST)
    target = iota(shape, 0)
    source = (target // LAST) * (ES * LAST) + target % LAST
    last = received_ref[:, ES * MAIN :, :].astype(F32)
    last = last.reshape(CHIPS * ES * LAST, quarter).astype(BF16)
    for q in range(ES):
        main = received_ref[:, q * MAIN : (q + 1) * MAIN, :].reshape(CHIPS * MAIN, quarter)
        pick = (iota(shape, 1) == source + q * LAST).astype(BF16)
        rows = jnp.concatenate([main, dot(pick, last).astype(BF16)], axis=0)
        gate = gate + dot(rows, gate_ref[q * quarter : (q + 1) * quarter, :])
        up = up + dot(rows, up_ref[q * quarter : (q + 1) * quarter, :])
    hidden_ref[...] = (jax.nn.silu(gate) * up).astype(BF16)


def hidden_units(received, gate_cols, up_cols):
    count = CHIPS * (MAIN + LAST)
    features, width = gate_cols.shape
    return pl.pallas_call(
        hidden_kernel,
        out_shape=jax.ShapeDtypeStruct((count, width), BF16),
        compiler_params=pltpu.CompilerParams(vmem_limit_bytes=VMEM_LIMIT),
        cost_estimate=pl.CostEstimate(
            flops=4 * count * features * width,
            bytes_accessed=4 * features * width + 2 * count * features,
            transcendentals=count * width,
        ),
    )(received, gate_cols, up_cols)


def down_kernel(pieces, mine_ref, theirs_ref, *refs):
    down_refs, other_refs, back_ref = refs[:pieces], refs[pieces : 2 * pieces], refs[2 * pieces]
    quarter = back_ref.shape[2]
    shape = (CHIPS * ES * LAST, CHIPS * LAST)
    row = iota(shape, 0)
    source = iota(shape, 1)
    last = jnp.zeros((CHIPS * ES * LAST, quarter), F32)
    for q in range(ES):
        columns = slice(q * quarter, (q + 1) * quarter)
        total = jnp.zeros((mine_ref.shape[0], quarter), F32)
        for hidden_ref, weights in ((mine_ref, down_refs), (theirs_ref, other_refs)):
            block = jnp.concatenate([ref[:, columns] for ref in weights], axis=0)
            total = total + dot(hidden_ref[...], block)
        total = total.astype(BF16)
        for chip in range(CHIPS):
            back_ref[chip, q * MAIN : (q + 1) * MAIN, :] = total[chip * MAIN : (chip + 1) * MAIN]
        inside = row % (ES * LAST) - q * LAST
        pick = (inside >= 0) & (inside < LAST)
        pick = pick & (source == (row // (ES * LAST)) * LAST + inside)
        last = last + dot(pick.astype(BF16), total[CHIPS * MAIN :])
    for chip in range(CHIPS):
        rows = last[chip * ES * LAST : (chip + 1) * ES * LAST]
        back_ref[chip, ES * MAIN :, :] = rows.astype(BF16)


def down_product(mine, theirs, down, other_down):
    count, width = mine.shape
    features = down[0].shape[1]
    return pl.pallas_call(
        functools.partial(down_kernel, len(down)),
        out_shape=jax.ShapeDtypeStruct((CHIPS, ES * (MAIN + LAST), features // ES), BF16),
        compiler_params=pltpu.CompilerParams(vmem_limit_bytes=VMEM_LIMIT),
        cost_estimate=pl.CostEstimate(
            flops=4 * count * width * features,
            bytes_accessed=4 * width * features + 2 * count * features,
            transcendentals=0,
        ),
    )(mine, theirs, *down, *other_down)


def finish_kernel(current_ref, back_ref, ids_ref, scores_ref, out_ref):
    tokens, features = current_ref.shape
    quarter = features // ES
    ids_row = ids_ref[...]
    ids_column = to_column(ids_row)
    score = to_column(scores_ref[...])
    earlier = (ids_column == ids_row) & (iota((tokens, tokens), 1) < iota((tokens, tokens), 0))
    slot = jnp.sum(earlier.astype(jnp.int32), axis=1, keepdims=True)
    lane = iota((tokens, CHIPS * MAIN), 1)
    pick_main = (lane // (2 * MAIN) == ids_column) & (lane % MAIN == slot)
    pick_main = pick_main.astype(BF16)
    lane = iota((tokens, CHIPS * ES * LAST), 1)
    in_expert = (lane // (2 * ES * LAST) == ids_column) & (slot >= MAIN)
    in_block = lane % (ES * LAST)
    last = jnp.concatenate(
        [back_ref[chip, ES * MAIN :, :].astype(F32) for chip in range(CHIPS)], axis=0
    ).astype(BF16)
    for q in range(ES):
        main = jnp.concatenate(
            [back_ref[chip, q * MAIN : (q + 1) * MAIN, :] for chip in range(CHIPS)], axis=0
        )
        pick_last = in_expert & (in_block == q * LAST + slot - MAIN)
        moe = (dot(pick_main, main) + dot(pick_last.astype(BF16), last)) * score
        columns = slice(q * quarter, (q + 1) * quarter)
        out_ref[:, columns] = (current_ref[:, columns].astype(F32) + moe).astype(BF16)


def finish(current, back, ids_row, scores_row):
    tokens, features = current.shape
    return pl.pallas_call(
        finish_kernel,
        out_shape=jax.ShapeDtypeStruct((tokens, features), BF16),
        compiler_params=pltpu.CompilerParams(vmem_limit_bytes=VMEM_LIMIT),
        cost_estimate=pl.CostEstimate(
            flops=6 * tokens * EXPERTS * MAIN * features,
            bytes_accessed=8 * tokens * features,
            transcendentals=0,
        ),
    )(current, back, ids_row, scores_row)


def settle_kernel(value_ref, out_ref):
    out_ref[...] = value_ref[...]


def settle(value):
    return pl.pallas_call(
        settle_kernel,
        out_shape=jax.ShapeDtypeStruct(value.shape, value.dtype),
        compiler_params=pltpu.CompilerParams(vmem_limit_bytes=VMEM_LIMIT),
        cost_estimate=pl.CostEstimate(flops=0, bytes_accessed=4 * value.size, transcendentals=0),
    )(value)


def swap_cores(value):
    return lax.ppermute(value, "ep", [(i, i ^ 1) for i in range(EP)])


def from_behind(value, steps):
    count = lax.axis_size("section")
    return lax.ppermute(value, "section", [(i, (i + steps) % count) for i in range(count)])


def behind_other_core(value, steps):
    count = lax.axis_size("section")
    pairs = [
        (s * EP + i, ((s + steps) % count) * EP + (i ^ 1)) for s in range(count) for i in range(EP)
    ]
    return lax.ppermute(value, ("section", "ep"), pairs)


def exchange(blocks):
    same_core = [[2 * chip + core for chip in range(CHIPS)] for core in range(2)]
    return lax.all_to_all(
        blocks, "ep", split_axis=0, concat_axis=0, axis_index_groups=same_core, tiled=True
    )


def on_device(
    flight_a, flight_b, routes_a, routes_b, scores_a, scores_b, norm_gain, w_gate, w_up, w_down
):
    tokens = flight_a.shape[1]
    current_a, current_b = flight_a[0], flight_b[0]
    ids_a, ids_b = routes_a.reshape(1, tokens), routes_b.reshape(1, tokens)
    marks_a, marks_b = scores_a.reshape(1, tokens), scores_b.reshape(1, tokens)
    gate_cols, up_cols, down = w_gate[0], w_up[0], w_down[0]

    own_a = exchange(prepare(current_a, ids_a, norm_gain, VMEM_WHOLE))
    other_down = swap_cores(down)
    staged_b, other_down = lax.optimization_barrier((current_b, other_down))
    send_b = prepare(staged_b, ids_b, norm_gain, VMEM_LIMIT)
    middle = down.shape[0] // 2
    upper = from_behind(down[:middle], -1)
    own_a, send_b, upper = lax.optimization_barrier((own_a, send_b, upper))
    own_b = exchange(send_b)

    lower = from_behind(down[middle:], -1)
    mine_a = hidden_units(own_a, gate_cols, up_cols)
    give_a = hidden_units(swap_cores(own_a), gate_cols, up_cols)
    back_a = down_product(mine_a, swap_cores(give_a), [down], [other_down])
    own_b, back_a, lower = lax.optimization_barrier((own_b, back_a, lower))

    returned_a = exchange(back_a)
    mine_b = hidden_units(own_b, gate_cols, up_cols)
    give_b = hidden_units(swap_cores(own_b), gate_cols, up_cols)
    moved_down = [upper, lower]
    back_b = down_product(
        from_behind(mine_b, -1),
        behind_other_core(give_b, -1),
        moved_down,
        [swap_cores(piece) for piece in moved_down],
    )
    moved_b, moved_ids, moved_marks = [
        from_behind(value, -1) for value in (current_b, ids_b, marks_b)
    ]

    marks_a, back_b = lax.optimization_barrier((marks_a, back_b))
    returned_b = exchange(back_b)
    updated_a = settle(from_behind(finish(current_a, returned_a, ids_a, marks_a), 1))
    updated_b = finish(moved_b, returned_b, moved_ids, moved_marks)
    return (updated_a[None], updated_b[None])


def solution(mesh):
    placed = (
        P("section", "ep", None),
        P("section", "ep", None),
        P("section", None, "ep", None),
        P("section", None, "ep", None),
        P("section", None, "ep", None),
        P("section", None, "ep", None),
        P("section", None),
        P("section", None, "ep"),
        P("section", None, "ep"),
        P("section", "ep", None),
    )
    return jax.shard_map(
        on_device,
        mesh=mesh,
        in_specs=placed,
        out_specs=(P("section", "ep", None), P("section", "ep", None)),
        check_vma=False,
    )
```

```python
import functools

import jax
import jax.numpy as jnp
from jax import lax
from jax.experimental import pallas as pl
from jax.experimental.pallas import tpu as pltpu
from jax.sharding import PartitionSpec as P

ES = 4
EXPERTS = 8
EP = ES * EXPERTS
CHIPS = EP // 2
MAIN = 16
LAST = 2
EPSILON = 1e-06
F32 = jnp.float32
BF16 = jnp.bfloat16
VMEM_LIMIT = 20 * 1024 * 1024
VMEM_WHOLE = 64 * 1024 * 1024 - 512 * 1024


def iota(shape, axis):
    return lax.broadcasted_iota(jnp.int32, shape, axis)


def to_column(row):
    count = row.shape[1]
    eye = iota((count, count), 0) == iota((count, count), 1)
    return jnp.sum(jnp.where(eye, row, jnp.zeros_like(row)), axis=1, keepdims=True)


def dot(left, right):
    return jnp.dot(left, right, preferred_element_type=F32)


def prepare_kernel(
    current_hbm, ids_hbm, gain_hbm, send_hbm,
    current_ref, ids_ref, gain_ref, normed_ref, send_ref, ready, done,
):
    loads = [
        pltpu.make_async_copy(source, target, ready.at[place])
        for place, (source, target) in enumerate(
            ((ids_hbm, ids_ref), (current_hbm, current_ref), (gain_hbm, gain_ref))
        )
    ]
    for load in loads:
        load.start()
    tokens, features = current_ref.shape
    quarter = features // ES
    loads[0].wait()
    ids_row = ids_ref[...]
    ids_column = to_column(ids_row)
    same = ids_column == ids_row
    earlier = same & (iota((tokens, tokens), 0) < iota((tokens, tokens), 1))
    slot_row = jnp.sum(earlier.astype(jnp.int32), axis=0, keepdims=True)
    main_row = jnp.where(slot_row < MAIN, ids_row * MAIN + slot_row, -1)
    last_row = jnp.where(slot_row < MAIN, -1, ids_row * (ES * LAST) + slot_row - MAIN)
    loads[1].wait()
    loads[2].wait()
    as_float = current_ref[...].astype(F32)
    inverse_rms = lax.rsqrt(jnp.mean(as_float * as_float, axis=-1, keepdims=True) + EPSILON)
    group = EXPERTS // 2
    stores = []
    for half in range(2):
        first = half * group
        pick_main = iota((group * MAIN, tokens), 0) + first * MAIN == main_row
        pick_main = pick_main.astype(BF16)
        last = jnp.zeros((group * ES * LAST, quarter), F32)
        for q in range(ES):
            columns = slice(q * quarter, (q + 1) * quarter)
            if half == 0:
                normed = current_ref[:, columns].astype(F32) * inverse_rms * gain_ref[:, columns]
                normed_ref[:, columns] = normed.astype(BF16)
            normed = normed_ref[:, columns]
            main = dot(pick_main, normed).astype(BF16)
            for expert in range(group):
                rows = main[expert * MAIN : (expert + 1) * MAIN]
                for chip in (2 * (first + expert), 2 * (first + expert) + 1):
                    send_ref[chip, q * MAIN : (q + 1) * MAIN, :] = rows
            place = jnp.where(last_row < 0, -1, last_row + q * LAST)
            pick_last = iota((group * ES * LAST, tokens), 0) + first * ES * LAST == place
            last = last + dot(pick_last.astype(BF16), normed)
        for expert in range(group):
            rows = last[expert * ES * LAST : (expert + 1) * ES * LAST].astype(BF16)
            for chip in (2 * (first + expert), 2 * (first + expert) + 1):
                send_ref[chip, ES * MAIN :, :] = rows
        part = pl.ds(2 * first, 2 * group)
        stores.append(pltpu.make_async_copy(send_ref.at[part], send_hbm.at[part], done.at[half]))
        stores[half].start()
    for store in stores:
        store.wait()


def prepare(current, ids_row, gain, vmem):
    tokens, features = current.shape
    quarter = features // ES
    return pl.pallas_call(
        prepare_kernel,
        out_shape=jax.ShapeDtypeStruct((CHIPS, ES * (MAIN + LAST), quarter), BF16),
        in_specs=[pl.BlockSpec(memory_space=pltpu.HBM)] * 3,
        out_specs=pl.BlockSpec(memory_space=pltpu.HBM),
        scratch_shapes=[
            pltpu.VMEM(current.shape, current.dtype),
            pltpu.VMEM(ids_row.shape, ids_row.dtype),
            pltpu.VMEM(gain.shape, gain.dtype),
            pltpu.VMEM(current.shape, BF16),
            pltpu.VMEM((CHIPS, ES * (MAIN + LAST), quarter), BF16),
            pltpu.SemaphoreType.DMA((3,)),
            pltpu.SemaphoreType.DMA((2,)),
        ],
        compiler_params=pltpu.CompilerParams(vmem_limit_bytes=vmem),
        cost_estimate=pl.CostEstimate(
            flops=3 * tokens * tokens * features, bytes_accessed=8 * tokens * features, transcendentals=0
        ),
    )(current, ids_row, gain)


def hidden_kernel(received_ref, gate_ref, up_ref, hidden_ref):
    quarter = received_ref.shape[2]
    count = CHIPS * (MAIN + LAST)
    gate = jnp.zeros((count, gate_ref.shape[1]), F32)
    up = jnp.zeros((count, up_ref.shape[1]), F32)
    shape = (CHIPS * LAST, CHIPS * ES * LAST)
    target = iota(shape, 0)
    source = (target // LAST) * (ES * LAST) + target % LAST
    last = received_ref[:, ES * MAIN :, :].astype(F32)
    last = last.reshape(CHIPS * ES * LAST, quarter).astype(BF16)
    for q in range(ES):
        main = received_ref[:, q * MAIN : (q + 1) * MAIN, :].reshape(CHIPS * MAIN, quarter)
        pick = (iota(shape, 1) == source + q * LAST).astype(BF16)
        rows = jnp.concatenate([main, dot(pick, last).astype(BF16)], axis=0)
        gate = gate + dot(rows, gate_ref[q * quarter : (q + 1) * quarter, :])
        up = up + dot(rows, up_ref[q * quarter : (q + 1) * quarter, :])
    hidden_ref[...] = (jax.nn.silu(gate) * up).astype(BF16)


def hidden_units(received, gate_cols, up_cols):
    count = CHIPS * (MAIN + LAST)
    features, width = gate_cols.shape
    return pl.pallas_call(
        hidden_kernel,
        out_shape=jax.ShapeDtypeStruct((count, width), BF16),
        compiler_params=pltpu.CompilerParams(vmem_limit_bytes=VMEM_LIMIT),
        cost_estimate=pl.CostEstimate(
            flops=4 * count * features * width,
            bytes_accessed=4 * features * width + 2 * count * features,
            transcendentals=count * width,
        ),
    )(received, gate_cols, up_cols)


def down_kernel(pieces, mine_ref, theirs_ref, *refs):
    down_refs, other_refs, back_ref = refs[:pieces], refs[pieces : 2 * pieces], refs[2 * pieces]
    quarter = back_ref.shape[2]
    shape = (CHIPS * ES * LAST, CHIPS * LAST)
    row = iota(shape, 0)
    source = iota(shape, 1)
    last = jnp.zeros((CHIPS * ES * LAST, quarter), F32)
    for q in range(ES):
        columns = slice(q * quarter, (q + 1) * quarter)
        total = jnp.zeros((mine_ref.shape[0], quarter), F32)
        for hidden_ref, weights in ((mine_ref, down_refs), (theirs_ref, other_refs)):
            block = jnp.concatenate([ref[:, columns] for ref in weights], axis=0)
            total = total + dot(hidden_ref[...], block)
        total = total.astype(BF16)
        for chip in range(CHIPS):
            back_ref[chip, q * MAIN : (q + 1) * MAIN, :] = total[chip * MAIN : (chip + 1) * MAIN]
        inside = row % (ES * LAST) - q * LAST
        pick = (inside >= 0) & (inside < LAST)
        pick = pick & (source == (row // (ES * LAST)) * LAST + inside)
        last = last + dot(pick.astype(BF16), total[CHIPS * MAIN :])
    for chip in range(CHIPS):
        rows = last[chip * ES * LAST : (chip + 1) * ES * LAST]
        back_ref[chip, ES * MAIN :, :] = rows.astype(BF16)


def down_product(mine, theirs, down, other_down):
    count, width = mine.shape
    features = down[0].shape[1]
    return pl.pallas_call(
        functools.partial(down_kernel, len(down)),
        out_shape=jax.ShapeDtypeStruct((CHIPS, ES * (MAIN + LAST), features // ES), BF16),
        compiler_params=pltpu.CompilerParams(vmem_limit_bytes=VMEM_LIMIT),
        cost_estimate=pl.CostEstimate(
            flops=4 * count * width * features,
            bytes_accessed=4 * width * features + 2 * count * features,
            transcendentals=0,
        ),
    )(mine, theirs, *down, *other_down)


def finish_kernel(current_ref, back_ref, ids_ref, scores_ref, out_ref):
    tokens, features = current_ref.shape
    quarter = features // ES
    ids_row = ids_ref[...]
    ids_column = to_column(ids_row)
    score = to_column(scores_ref[...])
    earlier = (ids_column == ids_row) & (iota((tokens, tokens), 1) < iota((tokens, tokens), 0))
    slot = jnp.sum(earlier.astype(jnp.int32), axis=1, keepdims=True)
    lane = iota((tokens, CHIPS * MAIN), 1)
    pick_main = (lane // (2 * MAIN) == ids_column) & (lane % MAIN == slot)
    pick_main = pick_main.astype(BF16)
    lane = iota((tokens, CHIPS * ES * LAST), 1)
    in_expert = (lane // (2 * ES * LAST) == ids_column) & (slot >= MAIN)
    in_block = lane % (ES * LAST)
    last = jnp.concatenate(
        [back_ref[chip, ES * MAIN :, :].astype(F32) for chip in range(CHIPS)], axis=0
    ).astype(BF16)
    for q in range(ES):
        main = jnp.concatenate(
            [back_ref[chip, q * MAIN : (q + 1) * MAIN, :] for chip in range(CHIPS)], axis=0
        )
        pick_last = in_expert & (in_block == q * LAST + slot - MAIN)
        moe = (dot(pick_main, main) + dot(pick_last.astype(BF16), last)) * score
        columns = slice(q * quarter, (q + 1) * quarter)
        out_ref[:, columns] = (current_ref[:, columns].astype(F32) + moe).astype(BF16)


def finish(current, back, ids_row, scores_row):
    tokens, features = current.shape
    return pl.pallas_call(
        finish_kernel,
        out_shape=jax.ShapeDtypeStruct((tokens, features), BF16),
        compiler_params=pltpu.CompilerParams(vmem_limit_bytes=VMEM_LIMIT),
        cost_estimate=pl.CostEstimate(
            flops=6 * tokens * EXPERTS * MAIN * features,
            bytes_accessed=8 * tokens * features,
            transcendentals=0,
        ),
    )(current, back, ids_row, scores_row)


def finish_both_kernel(
    moved_hbm, current_ref, back_ref, ids_ref, scores_ref, settled_hbm, out_ref, done
):
    copy = pltpu.make_async_copy(moved_hbm, settled_hbm, done)
    copy.start()
    finish_kernel(current_ref, back_ref, ids_ref, scores_ref, out_ref)
    copy.wait()


def finish_both(moved, current, back, ids_row, scores_row):
    tokens, features = current.shape
    return pl.pallas_call(
        finish_both_kernel,
        out_shape=[jax.ShapeDtypeStruct((tokens, features), BF16)] * 2,
        in_specs=[pl.BlockSpec(memory_space=pltpu.HBM)]
        + [pl.BlockSpec(memory_space=pltpu.VMEM)] * 4,
        out_specs=[pl.BlockSpec(memory_space=pltpu.HBM), pl.BlockSpec(memory_space=pltpu.VMEM)],
        scratch_shapes=[pltpu.SemaphoreType.DMA],
        compiler_params=pltpu.CompilerParams(vmem_limit_bytes=VMEM_LIMIT),
        cost_estimate=pl.CostEstimate(
            flops=6 * tokens * EXPERTS * MAIN * features,
            bytes_accessed=12 * tokens * features,
            transcendentals=0,
        ),
    )(moved, current, back, ids_row, scores_row)


def swap_cores(value):
    return lax.ppermute(value, "ep", [(i, i ^ 1) for i in range(EP)])


def from_behind(value, steps):
    count = lax.axis_size("section")
    return lax.ppermute(value, "section", [(i, (i + steps) % count) for i in range(count)])


def behind_other_core(value, steps):
    count = lax.axis_size("section")
    pairs = [
        (s * EP + i, ((s + steps) % count) * EP + (i ^ 1)) for s in range(count) for i in range(EP)
    ]
    return lax.ppermute(value, ("section", "ep"), pairs)


def exchange(blocks):
    same_core = [[2 * chip + core for chip in range(CHIPS)] for core in range(2)]
    return lax.all_to_all(
        blocks, "ep", split_axis=0, concat_axis=0, axis_index_groups=same_core, tiled=True
    )


def on_device(
    flight_a, flight_b, routes_a, routes_b, scores_a, scores_b, norm_gain, w_gate, w_up, w_down
):
    tokens = flight_a.shape[1]
    current_a, current_b = flight_a[0], flight_b[0]
    ids_a, ids_b = routes_a.reshape(1, tokens), routes_b.reshape(1, tokens)
    marks_a, marks_b = scores_a.reshape(1, tokens), scores_b.reshape(1, tokens)
    gate_cols, up_cols, down = w_gate[0], w_up[0], w_down[0]

    own_a = exchange(prepare(current_a, ids_a, norm_gain, VMEM_WHOLE))
    other_down = swap_cores(down)
    staged_b, other_down = lax.optimization_barrier((current_b, other_down))
    send_b = prepare(staged_b, ids_b, norm_gain, VMEM_LIMIT)
    middle = down.shape[0] // 2
    upper = from_behind(down[:middle], -1)
    own_a, send_b, upper = lax.optimization_barrier((own_a, send_b, upper))
    own_b = exchange(send_b)

    lower = from_behind(down[middle:], -1)
    mine_a = hidden_units(own_a, gate_cols, up_cols)
    give_a = hidden_units(swap_cores(own_a), gate_cols, up_cols)
    back_a = down_product(mine_a, swap_cores(give_a), [down], [other_down])
    own_b, back_a, lower = lax.optimization_barrier((own_b, back_a, lower))

    returned_a = exchange(back_a)
    mine_b = hidden_units(own_b, gate_cols, up_cols)
    give_b = hidden_units(swap_cores(own_b), gate_cols, up_cols)
    moved_down = [upper, lower]
    back_b = down_product(
        from_behind(mine_b, -1),
        behind_other_core(give_b, -1),
        moved_down,
        [swap_cores(piece) for piece in moved_down],
    )
    moved_b, moved_ids, moved_marks = [
        from_behind(value, -1) for value in (current_b, ids_b, marks_b)
    ]

    marks_a, back_b = lax.optimization_barrier((marks_a, back_b))
    returned_b = exchange(back_b)
    updated_a = from_behind(finish(current_a, returned_a, ids_a, marks_a), 1)
    updated_a, updated_b = finish_both(updated_a, moved_b, returned_b, moved_ids, moved_marks)
    return (updated_a[None], updated_b[None])


def solution(mesh):
    placed = (
        P("section", "ep", None),
        P("section", "ep", None),
        P("section", None, "ep", None),
        P("section", None, "ep", None),
        P("section", None, "ep", None),
        P("section", None, "ep", None),
        P("section", None),
        P("section", None, "ep"),
        P("section", None, "ep"),
        P("section", "ep", None),
    )
    return jax.shard_map(
        on_device,
        mesh=mesh,
        in_specs=placed,
        out_specs=(P("section", "ep", None), P("section", "ep", None)),
        check_vma=False,
    )
```

```python
import functools

import jax
import jax.numpy as jnp
from jax import lax
from jax.experimental import pallas as pl
from jax.experimental.pallas import tpu as pltpu
from jax.sharding import PartitionSpec as P

ES = 4
EXPERTS = 8
EP = ES * EXPERTS
CHIPS = EP // 2
MAIN = 16
LAST = 2
ORDER = (0, 1, 2, 3, 5, 6, 7, 4, 10, 11, 8, 9, 15, 12, 13, 14)
EPSILON = 1e-06
F32 = jnp.float32
BF16 = jnp.bfloat16
VMEM_LIMIT = 20 * 1024 * 1024
VMEM_WHOLE = 64 * 1024 * 1024 - 512 * 1024


def iota(shape, axis):
    return lax.broadcasted_iota(jnp.int32, shape, axis)


def to_column(row):
    count = row.shape[1]
    eye = iota((count, count), 0) == iota((count, count), 1)
    return jnp.sum(jnp.where(eye, row, jnp.zeros_like(row)), axis=1, keepdims=True)


def dot(left, right):
    return jnp.dot(left, right, preferred_element_type=F32)


def prepare_kernel(current_hbm, ids_hbm, gain_hbm, send_ref, current_ref, ids_ref, gain_ref, ready):
    loads = [
        pltpu.make_async_copy(source, target, ready.at[place])
        for place, (source, target) in enumerate(
            ((ids_hbm, ids_ref), (current_hbm, current_ref), (gain_hbm, gain_ref))
        )
    ]
    for load in loads:
        load.start()
    tokens, features = current_ref.shape
    quarter = features // ES
    loads[0].wait()
    ids_row = ids_ref[...]
    ids_column = to_column(ids_row)
    same = ids_column == ids_row
    earlier = same & (iota((tokens, tokens), 0) < iota((tokens, tokens), 1))
    slot_row = jnp.sum(earlier.astype(jnp.int32), axis=0, keepdims=True)
    main_row = jnp.where(slot_row < MAIN, ids_row * MAIN + slot_row, -1)
    last_row = jnp.where(slot_row < MAIN, -1, ids_row * (ES * LAST) + slot_row - MAIN)
    pick_main = (iota((EXPERTS * MAIN, tokens), 0) == main_row).astype(BF16)
    loads[1].wait()
    loads[2].wait()
    as_float = current_ref[...].astype(F32)
    inverse_rms = lax.rsqrt(jnp.mean(as_float * as_float, axis=-1, keepdims=True) + EPSILON)
    last = jnp.zeros((EXPERTS * ES * LAST, quarter), F32)
    for q in range(ES):
        columns = slice(q * quarter, (q + 1) * quarter)
        normed = (current_ref[:, columns].astype(F32) * inverse_rms * gain_ref[:, columns]).astype(
            BF16
        )
        main = dot(pick_main, normed).astype(BF16)
        for expert in range(EXPERTS):
            rows = main[expert * MAIN : (expert + 1) * MAIN]
            for chip in (2 * expert, 2 * expert + 1):
                send_ref[ORDER.index(chip), q * MAIN : (q + 1) * MAIN, :] = rows
        place = jnp.where(last_row < 0, -1, last_row + q * LAST)
        pick_last = (iota((EXPERTS * ES * LAST, tokens), 0) == place).astype(BF16)
        last = last + dot(pick_last, normed)
    for expert in range(EXPERTS):
        rows = last[expert * ES * LAST : (expert + 1) * ES * LAST].astype(BF16)
        for chip in (2 * expert, 2 * expert + 1):
            send_ref[ORDER.index(chip), ES * MAIN :, :] = rows


def prepare(current, ids_row, gain, vmem):
    tokens, features = current.shape
    quarter = features // ES
    return pl.pallas_call(
        prepare_kernel,
        out_shape=jax.ShapeDtypeStruct((CHIPS, ES * (MAIN + LAST), quarter), BF16),
        in_specs=[pl.BlockSpec(memory_space=pltpu.HBM)] * 3,
        scratch_shapes=[
            pltpu.VMEM(current.shape, current.dtype),
            pltpu.VMEM(ids_row.shape, ids_row.dtype),
            pltpu.VMEM(gain.shape, gain.dtype),
            pltpu.SemaphoreType.DMA((3,)),
        ],
        compiler_params=pltpu.CompilerParams(vmem_limit_bytes=vmem),
        cost_estimate=pl.CostEstimate(
            flops=3 * tokens * tokens * features, bytes_accessed=8 * tokens * features, transcendentals=0
        ),
    )(current, ids_row, gain)


def hidden_kernel(received_ref, gate_ref, up_ref, hidden_ref):
    quarter = received_ref.shape[2]
    count = CHIPS * (MAIN + LAST)
    gate = jnp.zeros((count, gate_ref.shape[1]), F32)
    up = jnp.zeros((count, up_ref.shape[1]), F32)
    shape = (CHIPS * LAST, CHIPS * ES * LAST)
    target = iota(shape, 0)
    source = (target // LAST) * (ES * LAST) + target % LAST
    last = received_ref[:, ES * MAIN :, :].astype(F32)
    last = last.reshape(CHIPS * ES * LAST, quarter).astype(BF16)
    for q in range(ES):
        main = received_ref[:, q * MAIN : (q + 1) * MAIN, :].reshape(CHIPS * MAIN, quarter)
        pick = (iota(shape, 1) == source + q * LAST).astype(BF16)
        rows = jnp.concatenate([main, dot(pick, last).astype(BF16)], axis=0)
        gate = gate + dot(rows, gate_ref[q * quarter : (q + 1) * quarter, :])
        up = up + dot(rows, up_ref[q * quarter : (q + 1) * quarter, :])
    hidden_ref[...] = (jax.nn.silu(gate) * up).astype(BF16)


def hidden_units(received, gate_cols, up_cols):
    count = CHIPS * (MAIN + LAST)
    features, width = gate_cols.shape
    return pl.pallas_call(
        hidden_kernel,
        out_shape=jax.ShapeDtypeStruct((count, width), BF16),
        compiler_params=pltpu.CompilerParams(vmem_limit_bytes=VMEM_LIMIT),
        cost_estimate=pl.CostEstimate(
            flops=4 * count * features * width,
            bytes_accessed=4 * features * width + 2 * count * features,
            transcendentals=count * width,
        ),
    )(received, gate_cols, up_cols)


def down_kernel(pieces, mine_ref, theirs_ref, *refs):
    down_refs, other_refs, back_ref = refs[:pieces], refs[pieces : 2 * pieces], refs[2 * pieces]
    quarter = back_ref.shape[2]
    shape = (CHIPS * ES * LAST, CHIPS * LAST)
    row = iota(shape, 0)
    source = iota(shape, 1)
    last = jnp.zeros((CHIPS * ES * LAST, quarter), F32)
    for q in range(ES):
        columns = slice(q * quarter, (q + 1) * quarter)
        total = jnp.zeros((mine_ref.shape[0], quarter), F32)
        for hidden_ref, weights in ((mine_ref, down_refs), (theirs_ref, other_refs)):
            block = jnp.concatenate([ref[:, columns] for ref in weights], axis=0)
            total = total + dot(hidden_ref[...], block)
        total = total.astype(BF16)
        for chip in range(CHIPS):
            back_ref[chip, q * MAIN : (q + 1) * MAIN, :] = total[chip * MAIN : (chip + 1) * MAIN]
        inside = row % (ES * LAST) - q * LAST
        pick = (inside >= 0) & (inside < LAST)
        pick = pick & (source == (row // (ES * LAST)) * LAST + inside)
        last = last + dot(pick.astype(BF16), total[CHIPS * MAIN :])
    for chip in range(CHIPS):
        rows = last[chip * ES * LAST : (chip + 1) * ES * LAST]
        back_ref[chip, ES * MAIN :, :] = rows.astype(BF16)


def down_product(mine, theirs, down, other_down):
    count, width = mine.shape
    features = down[0].shape[1]
    return pl.pallas_call(
        functools.partial(down_kernel, len(down)),
        out_shape=jax.ShapeDtypeStruct((CHIPS, ES * (MAIN + LAST), features // ES), BF16),
        compiler_params=pltpu.CompilerParams(vmem_limit_bytes=VMEM_LIMIT),
        cost_estimate=pl.CostEstimate(
            flops=4 * count * width * features,
            bytes_accessed=4 * width * features + 2 * count * features,
            transcendentals=0,
        ),
    )(mine, theirs, *down, *other_down)


def finish_kernel(current_ref, back_ref, ids_ref, scores_ref, out_ref):
    tokens, features = current_ref.shape
    quarter = features // ES
    ids_row = ids_ref[...]
    ids_column = to_column(ids_row)
    score = to_column(scores_ref[...])
    earlier = (ids_column == ids_row) & (iota((tokens, tokens), 1) < iota((tokens, tokens), 0))
    slot = jnp.sum(earlier.astype(jnp.int32), axis=1, keepdims=True)
    lane = iota((tokens, CHIPS * MAIN), 1)
    pick_main = (lane // (2 * MAIN) == ids_column) & (lane % MAIN == slot)
    pick_main = pick_main.astype(BF16)
    lane = iota((tokens, CHIPS * ES * LAST), 1)
    in_expert = (lane // (2 * ES * LAST) == ids_column) & (slot >= MAIN)
    in_block = lane % (ES * LAST)
    last = jnp.concatenate(
        [back_ref[ORDER.index(chip), ES * MAIN :, :].astype(F32) for chip in range(CHIPS)], axis=0
    ).astype(BF16)
    for q in range(ES):
        main = jnp.concatenate(
            [back_ref[ORDER.index(chip), q * MAIN : (q + 1) * MAIN, :] for chip in range(CHIPS)], axis=0
        )
        pick_last = in_expert & (in_block == q * LAST + slot - MAIN)
        moe = (dot(pick_main, main) + dot(pick_last.astype(BF16), last)) * score
        columns = slice(q * quarter, (q + 1) * quarter)
        out_ref[:, columns] = (current_ref[:, columns].astype(F32) + moe).astype(BF16)


def finish(current, back, ids_row, scores_row):
    tokens, features = current.shape
    return pl.pallas_call(
        finish_kernel,
        out_shape=jax.ShapeDtypeStruct((tokens, features), BF16),
        compiler_params=pltpu.CompilerParams(vmem_limit_bytes=VMEM_LIMIT),
        cost_estimate=pl.CostEstimate(
            flops=6 * tokens * EXPERTS * MAIN * features,
            bytes_accessed=8 * tokens * features,
            transcendentals=0,
        ),
    )(current, back, ids_row, scores_row)


def settle_kernel(value_ref, out_ref):
    out_ref[...] = value_ref[...]


def settle(value):
    return pl.pallas_call(
        settle_kernel,
        out_shape=jax.ShapeDtypeStruct(value.shape, value.dtype),
        compiler_params=pltpu.CompilerParams(vmem_limit_bytes=VMEM_LIMIT),
        cost_estimate=pl.CostEstimate(flops=0, bytes_accessed=4 * value.size, transcendentals=0),
    )(value)


def swap_cores(value):
    return lax.ppermute(value, "ep", [(i, i ^ 1) for i in range(EP)])


def from_behind(value, steps):
    count = lax.axis_size("section")
    return lax.ppermute(value, "section", [(i, (i + steps) % count) for i in range(count)])


def behind_other_core(value, steps):
    count = lax.axis_size("section")
    pairs = [
        (s * EP + i, ((s + steps) % count) * EP + (i ^ 1)) for s in range(count) for i in range(EP)
    ]
    return lax.ppermute(value, ("section", "ep"), pairs)


def exchange(blocks):
    same_core = [[2 * chip + core for chip in ORDER] for core in range(2)]
    return lax.all_to_all(
        blocks, "ep", split_axis=0, concat_axis=0, axis_index_groups=same_core, tiled=True
    )


def on_device(
    flight_a, flight_b, routes_a, routes_b, scores_a, scores_b, norm_gain, w_gate, w_up, w_down
):
    tokens = flight_a.shape[1]
    current_a, current_b = flight_a[0], flight_b[0]
    ids_a, ids_b = routes_a.reshape(1, tokens), routes_b.reshape(1, tokens)
    marks_a, marks_b = scores_a.reshape(1, tokens), scores_b.reshape(1, tokens)
    gate_cols, up_cols, down = w_gate[0], w_up[0], w_down[0]

    own_a = exchange(prepare(current_a, ids_a, norm_gain, VMEM_WHOLE))
    other_down = swap_cores(down)
    staged_b, other_down = lax.optimization_barrier((current_b, other_down))
    send_b = prepare(staged_b, ids_b, norm_gain, VMEM_LIMIT)
    middle = down.shape[0] // 2
    upper = from_behind(down[:middle], -1)
    own_a, send_b, upper = lax.optimization_barrier((own_a, send_b, upper))
    own_b = exchange(send_b)

    lower = from_behind(down[middle:], -1)
    mine_a = hidden_units(own_a, gate_cols, up_cols)
    give_a = hidden_units(swap_cores(own_a), gate_cols, up_cols)
    back_a = down_product(mine_a, swap_cores(give_a), [down], [other_down])
    own_b, back_a, lower = lax.optimization_barrier((own_b, back_a, lower))

    returned_a = exchange(back_a)
    mine_b = hidden_units(own_b, gate_cols, up_cols)
    give_b = hidden_units(swap_cores(own_b), gate_cols, up_cols)
    moved_down = [upper, lower]
    back_b = down_product(
        from_behind(mine_b, -1),
        behind_other_core(give_b, -1),
        moved_down,
        [swap_cores(piece) for piece in moved_down],
    )
    moved_b, moved_ids, moved_marks = [
        from_behind(value, -1) for value in (current_b, ids_b, marks_b)
    ]

    marks_a, back_b = lax.optimization_barrier((marks_a, back_b))
    returned_b = exchange(back_b)
    updated_a = settle(from_behind(finish(current_a, returned_a, ids_a, marks_a), 1))
    updated_b = finish(moved_b, returned_b, moved_ids, moved_marks)
    return (updated_a[None], updated_b[None])


def solution(mesh):
    placed = (
        P("section", "ep", None),
        P("section", "ep", None),
        P("section", None, "ep", None),
        P("section", None, "ep", None),
        P("section", None, "ep", None),
        P("section", None, "ep", None),
        P("section", None),
        P("section", None, "ep"),
        P("section", None, "ep"),
        P("section", "ep", None),
    )
    return jax.shard_map(
        on_device,
        mesh=mesh,
        in_specs=placed,
        out_specs=(P("section", "ep", None), P("section", "ep", None)),
        check_vma=False,
    )
```

```python
import functools

import jax
import jax.numpy as jnp
from jax import lax
from jax.experimental import pallas as pl
from jax.experimental.pallas import tpu as pltpu
from jax.sharding import PartitionSpec as P

ES = 4
EXPERTS = 8
EP = ES * EXPERTS
CHIPS = EP // 2
MAIN = 16
LAST = 2
ORDER = (0, 1, 2, 3, 7, 4, 5, 6, 10, 11, 8, 9, 13, 14, 15, 12)
EPSILON = 1e-06
F32 = jnp.float32
BF16 = jnp.bfloat16
VMEM_LIMIT = 20 * 1024 * 1024
VMEM_WHOLE = 64 * 1024 * 1024 - 512 * 1024


def iota(shape, axis):
    return lax.broadcasted_iota(jnp.int32, shape, axis)


def to_column(row):
    count = row.shape[1]
    eye = iota((count, count), 0) == iota((count, count), 1)
    return jnp.sum(jnp.where(eye, row, jnp.zeros_like(row)), axis=1, keepdims=True)


def dot(left, right):
    return jnp.dot(left, right, preferred_element_type=F32)


def prepare_kernel(current_hbm, ids_hbm, gain_hbm, send_ref, current_ref, ids_ref, gain_ref, ready):
    loads = [
        pltpu.make_async_copy(source, target, ready.at[place])
        for place, (source, target) in enumerate(
            ((ids_hbm, ids_ref), (current_hbm, current_ref), (gain_hbm, gain_ref))
        )
    ]
    for load in loads:
        load.start()
    tokens, features = current_ref.shape
    quarter = features // ES
    loads[0].wait()
    ids_row = ids_ref[...]
    ids_column = to_column(ids_row)
    same = ids_column == ids_row
    earlier = same & (iota((tokens, tokens), 0) < iota((tokens, tokens), 1))
    slot_row = jnp.sum(earlier.astype(jnp.int32), axis=0, keepdims=True)
    main_row = jnp.where(slot_row < MAIN, ids_row * MAIN + slot_row, -1)
    last_row = jnp.where(slot_row < MAIN, -1, ids_row * (ES * LAST) + slot_row - MAIN)
    pick_main = (iota((EXPERTS * MAIN, tokens), 0) == main_row).astype(BF16)
    loads[1].wait()
    loads[2].wait()
    as_float = current_ref[...].astype(F32)
    inverse_rms = lax.rsqrt(jnp.mean(as_float * as_float, axis=-1, keepdims=True) + EPSILON)
    last = jnp.zeros((EXPERTS * ES * LAST, quarter), F32)
    for q in range(ES):
        columns = slice(q * quarter, (q + 1) * quarter)
        normed = (current_ref[:, columns].astype(F32) * inverse_rms * gain_ref[:, columns]).astype(
            BF16
        )
        main = dot(pick_main, normed).astype(BF16)
        for expert in range(EXPERTS):
            rows = main[expert * MAIN : (expert + 1) * MAIN]
            for chip in (2 * expert, 2 * expert + 1):
                send_ref[ORDER.index(chip), q * MAIN : (q + 1) * MAIN, :] = rows
        place = jnp.where(last_row < 0, -1, last_row + q * LAST)
        pick_last = (iota((EXPERTS * ES * LAST, tokens), 0) == place).astype(BF16)
        last = last + dot(pick_last, normed)
    for expert in range(EXPERTS):
        rows = last[expert * ES * LAST : (expert + 1) * ES * LAST].astype(BF16)
        for chip in (2 * expert, 2 * expert + 1):
            send_ref[ORDER.index(chip), ES * MAIN :, :] = rows


def prepare(current, ids_row, gain, vmem):
    tokens, features = current.shape
    quarter = features // ES
    return pl.pallas_call(
        prepare_kernel,
        out_shape=jax.ShapeDtypeStruct((CHIPS, ES * (MAIN + LAST), quarter), BF16),
        in_specs=[pl.BlockSpec(memory_space=pltpu.HBM)] * 3,
        scratch_shapes=[
            pltpu.VMEM(current.shape, current.dtype),
            pltpu.VMEM(ids_row.shape, ids_row.dtype),
            pltpu.VMEM(gain.shape, gain.dtype),
            pltpu.SemaphoreType.DMA((3,)),
        ],
        compiler_params=pltpu.CompilerParams(vmem_limit_bytes=vmem),
        cost_estimate=pl.CostEstimate(
            flops=3 * tokens * tokens * features, bytes_accessed=8 * tokens * features, transcendentals=0
        ),
    )(current, ids_row, gain)


def hidden_kernel(received_ref, gate_ref, up_ref, hidden_ref):
    quarter = received_ref.shape[2]
    count = CHIPS * (MAIN + LAST)
    gate = jnp.zeros((count, gate_ref.shape[1]), F32)
    up = jnp.zeros((count, up_ref.shape[1]), F32)
    shape = (CHIPS * LAST, CHIPS * ES * LAST)
    target = iota(shape, 0)
    source = (target // LAST) * (ES * LAST) + target % LAST
    last = received_ref[:, ES * MAIN :, :].astype(F32)
    last = last.reshape(CHIPS * ES * LAST, quarter).astype(BF16)
    for q in range(ES):
        main = received_ref[:, q * MAIN : (q + 1) * MAIN, :].reshape(CHIPS * MAIN, quarter)
        pick = (iota(shape, 1) == source + q * LAST).astype(BF16)
        rows = jnp.concatenate([main, dot(pick, last).astype(BF16)], axis=0)
        gate = gate + dot(rows, gate_ref[q * quarter : (q + 1) * quarter, :])
        up = up + dot(rows, up_ref[q * quarter : (q + 1) * quarter, :])
    hidden_ref[...] = (jax.nn.silu(gate) * up).astype(BF16)


def hidden_units(received, gate_cols, up_cols):
    count = CHIPS * (MAIN + LAST)
    features, width = gate_cols.shape
    return pl.pallas_call(
        hidden_kernel,
        out_shape=jax.ShapeDtypeStruct((count, width), BF16),
        compiler_params=pltpu.CompilerParams(vmem_limit_bytes=VMEM_LIMIT),
        cost_estimate=pl.CostEstimate(
            flops=4 * count * features * width,
            bytes_accessed=4 * features * width + 2 * count * features,
            transcendentals=count * width,
        ),
    )(received, gate_cols, up_cols)


def down_kernel(pieces, mine_ref, theirs_ref, *refs):
    down_refs, other_refs, back_ref = refs[:pieces], refs[pieces : 2 * pieces], refs[2 * pieces]
    quarter = back_ref.shape[2]
    shape = (CHIPS * ES * LAST, CHIPS * LAST)
    row = iota(shape, 0)
    source = iota(shape, 1)
    last = jnp.zeros((CHIPS * ES * LAST, quarter), F32)
    for q in range(ES):
        columns = slice(q * quarter, (q + 1) * quarter)
        total = jnp.zeros((mine_ref.shape[0], quarter), F32)
        for hidden_ref, weights in ((mine_ref, down_refs), (theirs_ref, other_refs)):
            block = jnp.concatenate([ref[:, columns] for ref in weights], axis=0)
            total = total + dot(hidden_ref[...], block)
        total = total.astype(BF16)
        for chip in range(CHIPS):
            back_ref[chip, q * MAIN : (q + 1) * MAIN, :] = total[chip * MAIN : (chip + 1) * MAIN]
        inside = row % (ES * LAST) - q * LAST
        pick = (inside >= 0) & (inside < LAST)
        pick = pick & (source == (row // (ES * LAST)) * LAST + inside)
        last = last + dot(pick.astype(BF16), total[CHIPS * MAIN :])
    for chip in range(CHIPS):
        rows = last[chip * ES * LAST : (chip + 1) * ES * LAST]
        back_ref[chip, ES * MAIN :, :] = rows.astype(BF16)


def down_product(mine, theirs, down, other_down):
    count, width = mine.shape
    features = down[0].shape[1]
    return pl.pallas_call(
        functools.partial(down_kernel, len(down)),
        out_shape=jax.ShapeDtypeStruct((CHIPS, ES * (MAIN + LAST), features // ES), BF16),
        compiler_params=pltpu.CompilerParams(vmem_limit_bytes=VMEM_LIMIT),
        cost_estimate=pl.CostEstimate(
            flops=4 * count * width * features,
            bytes_accessed=4 * width * features + 2 * count * features,
            transcendentals=0,
        ),
    )(mine, theirs, *down, *other_down)


def finish_kernel(current_ref, back_ref, ids_ref, scores_ref, out_ref):
    tokens, features = current_ref.shape
    quarter = features // ES
    ids_row = ids_ref[...]
    ids_column = to_column(ids_row)
    score = to_column(scores_ref[...])
    earlier = (ids_column == ids_row) & (iota((tokens, tokens), 1) < iota((tokens, tokens), 0))
    slot = jnp.sum(earlier.astype(jnp.int32), axis=1, keepdims=True)
    lane = iota((tokens, CHIPS * MAIN), 1)
    pick_main = (lane // (2 * MAIN) == ids_column) & (lane % MAIN == slot)
    pick_main = pick_main.astype(BF16)
    lane = iota((tokens, CHIPS * ES * LAST), 1)
    in_expert = (lane // (2 * ES * LAST) == ids_column) & (slot >= MAIN)
    in_block = lane % (ES * LAST)
    last = jnp.concatenate(
        [back_ref[ORDER.index(chip), ES * MAIN :, :].astype(F32) for chip in range(CHIPS)], axis=0
    ).astype(BF16)
    for q in range(ES):
        main = jnp.concatenate(
            [back_ref[ORDER.index(chip), q * MAIN : (q + 1) * MAIN, :] for chip in range(CHIPS)], axis=0
        )
        pick_last = in_expert & (in_block == q * LAST + slot - MAIN)
        moe = (dot(pick_main, main) + dot(pick_last.astype(BF16), last)) * score
        columns = slice(q * quarter, (q + 1) * quarter)
        out_ref[:, columns] = (current_ref[:, columns].astype(F32) + moe).astype(BF16)


def finish(current, back, ids_row, scores_row):
    tokens, features = current.shape
    return pl.pallas_call(
        finish_kernel,
        out_shape=jax.ShapeDtypeStruct((tokens, features), BF16),
        compiler_params=pltpu.CompilerParams(vmem_limit_bytes=VMEM_LIMIT),
        cost_estimate=pl.CostEstimate(
            flops=6 * tokens * EXPERTS * MAIN * features,
            bytes_accessed=8 * tokens * features,
            transcendentals=0,
        ),
    )(current, back, ids_row, scores_row)


def settle_kernel(value_ref, out_ref):
    out_ref[...] = value_ref[...]


def settle(value):
    return pl.pallas_call(
        settle_kernel,
        out_shape=jax.ShapeDtypeStruct(value.shape, value.dtype),
        compiler_params=pltpu.CompilerParams(vmem_limit_bytes=VMEM_LIMIT),
        cost_estimate=pl.CostEstimate(flops=0, bytes_accessed=4 * value.size, transcendentals=0),
    )(value)


def swap_cores(value):
    return lax.ppermute(value, "ep", [(i, i ^ 1) for i in range(EP)])


def from_behind(value, steps):
    count = lax.axis_size("section")
    return lax.ppermute(value, "section", [(i, (i + steps) % count) for i in range(count)])


def behind_other_core(value, steps):
    count = lax.axis_size("section")
    pairs = [
        (s * EP + i, ((s + steps) % count) * EP + (i ^ 1)) for s in range(count) for i in range(EP)
    ]
    return lax.ppermute(value, ("section", "ep"), pairs)


def exchange(blocks):
    same_core = [[2 * chip + core for chip in ORDER] for core in range(2)]
    return lax.all_to_all(
        blocks, "ep", split_axis=0, concat_axis=0, axis_index_groups=same_core, tiled=True
    )


def on_device(
    flight_a, flight_b, routes_a, routes_b, scores_a, scores_b, norm_gain, w_gate, w_up, w_down
):
    tokens = flight_a.shape[1]
    current_a, current_b = flight_a[0], flight_b[0]
    ids_a, ids_b = routes_a.reshape(1, tokens), routes_b.reshape(1, tokens)
    marks_a, marks_b = scores_a.reshape(1, tokens), scores_b.reshape(1, tokens)
    gate_cols, up_cols, down = w_gate[0], w_up[0], w_down[0]

    own_a = exchange(prepare(current_a, ids_a, norm_gain, VMEM_WHOLE))
    other_down = swap_cores(down)
    staged_b, other_down = lax.optimization_barrier((current_b, other_down))
    send_b = prepare(staged_b, ids_b, norm_gain, VMEM_LIMIT)
    middle = down.shape[0] // 2
    upper = from_behind(down[:middle], -1)
    own_a, send_b, upper = lax.optimization_barrier((own_a, send_b, upper))
    own_b = exchange(send_b)

    lower = from_behind(down[middle:], -1)
    mine_a = hidden_units(own_a, gate_cols, up_cols)
    give_a = hidden_units(swap_cores(own_a), gate_cols, up_cols)
    back_a = down_product(mine_a, swap_cores(give_a), [down], [other_down])
    own_b, back_a, lower = lax.optimization_barrier((own_b, back_a, lower))

    returned_a = exchange(back_a)
    mine_b = hidden_units(own_b, gate_cols, up_cols)
    give_b = hidden_units(swap_cores(own_b), gate_cols, up_cols)
    moved_down = [upper, lower]
    back_b = down_product(
        from_behind(mine_b, -1),
        behind_other_core(give_b, -1),
        moved_down,
        [swap_cores(piece) for piece in moved_down],
    )
    moved_b, moved_ids, moved_marks = [
        from_behind(value, -1) for value in (current_b, ids_b, marks_b)
    ]

    marks_a, back_b = lax.optimization_barrier((marks_a, back_b))
    returned_b = exchange(back_b)
    updated_a = settle(from_behind(finish(current_a, returned_a, ids_a, marks_a), 1))
    updated_b = finish(moved_b, returned_b, moved_ids, moved_marks)
    return (updated_a[None], updated_b[None])


def solution(mesh):
    placed = (
        P("section", "ep", None),
        P("section", "ep", None),
        P("section", None, "ep", None),
        P("section", None, "ep", None),
        P("section", None, "ep", None),
        P("section", None, "ep", None),
        P("section", None),
        P("section", None, "ep"),
        P("section", None, "ep"),
        P("section", "ep", None),
    )
    return jax.shard_map(
        on_device,
        mesh=mesh,
        in_specs=placed,
        out_specs=(P("section", "ep", None), P("section", "ep", None)),
        check_vma=False,
    )
```
